512 devices in a mesh: seq: 128 (over z, y, x_hi), tp: 4 (over x_lo, core).
Axes of the slice: x: 4 (x_hi: 2, x_lo: 2; x = x_hi * 2 + x_lo), y: 8, z: 8, core: 2. Of those that a mesh axis runs over, the one named last changes fastest.
Arguments:
- queries: bfloat16 [32768, 1024], P('seq', 'tp'), may hold values from -6 to 6
- keys: bfloat16 [32768, 1024], P('seq', 'tp'), may hold values from -6 to 6
- values: bfloat16 [32768, 1024], P('seq', 'tp'), may hold values from -6 to 6
- out_weight: bfloat16 [1024, 1024], P('tp'), may hold values from -0.1875 to 0.1875
- out_grad: bfloat16 [32768, 1024], P('seq', 'tp'), may hold values from -6 to 6
- near_offsets: int32 [512, 3], P('seq'), may hold values from -2 to 2, as said below
- coupling: int32 [512, 16], P('seq'), may hold values from 0 to 127
Outputs:
- mixed: bfloat16 [32768, 1024], P('seq', 'tp')
- grad_queries: bfloat16 [32768, 1024], P('seq', 'tp')
- grad_keys: bfloat16 [32768, 1024], P('seq', 'tp')
- grad_values: bfloat16 [32768, 1024], P('seq', 'tp')
- grad_weight: float32 [1024, 1024], P('tp')
The draws below stay inside these ranges and needn't reach their ends.
Inputs may be any that keep to these rules, and one draw needn't show every extreme that they name: `near_offsets`: each block's row holds 0 and two different nonzero offsets.
All inputs are finite; a program needn't handle non-finite values.
Results may differ from the reference program's by a relative error of at most 0.017.
Values may be sent and summed in bfloat16 or wider, within the bound.
A program may use at most 64 MiB of HBM per device.

```python
import math
import jax
import jax.numpy as jnp
from jax import lax

D = 1024
HEADS = 16
HD = 64
NB = 64
GROUP = 4
C1 = 16
TOKENS = 32768
NBLK = 512
NSUP = 128


def draw_queries(key, part):
    key = jax.random.fold_in(key, 3)
    drawn_vals = jnp.clip(jax.random.normal(key, (TOKENS, D), jnp.float32), -6.0, 6.0)
    return drawn_vals.astype(jnp.bfloat16)


def draw_keys(key, part):
    key = jax.random.fold_in(key, 4)
    drawn_vals = jnp.clip(jax.random.normal(key, (TOKENS, D), jnp.float32), -6.0, 6.0)
    return drawn_vals.astype(jnp.bfloat16)


def draw_near_offsets(key, part):
    key = jax.random.fold_in(key, 5)
    ranks = jax.random.randint(key, (NBLK, 4), 0, 1 << 20) * 4 + jnp.arange(4, dtype=jnp.int32)
    picked = jnp.argsort(ranks, axis=1)[:, :2]
    offset_table = jnp.array([-2, -1, 1, 2], jnp.int32)
    paired = offset_table[picked]
    row_ids = jnp.arange(NBLK)[:, None]
    paired = jnp.where(row_ids == 0, jnp.array([-2, 2], jnp.int32)[None, :], paired)
    return jnp.concatenate([jnp.zeros((NBLK, 1), jnp.int32), paired], 1).astype(jnp.int32)


def place_ends(drawn, key, low, largest):
    extent = drawn.shape
    index_at = [jax.random.randint(jax.random.fold_in(key, axis), (), 0, extent[axis]) for axis in range(len(extent))]
    drawn = drawn.at[tuple(index_at)].set(low)
    longest = extent.index(max(extent))
    index_at[longest] = (index_at[longest] + 1) % extent[longest]
    return drawn.at[tuple(index_at)].set(largest)


def level_of(rng, dims, shards, smallest, largest):
    loudness, own = 1.0, jax.random.fold_in(rng, 6)
    for axis_at, shards_of in shards:
        heights = jnp.exp(jax.random.uniform(jax.random.fold_in(own, axis_at), (shards_of,), jnp.float32, smallest / len(shards), largest / len(shards)))
        loudness = loudness * jnp.repeat(heights, dims[axis_at] // shards_of).reshape([-1 if axis == axis_at else 1 for axis in range(len(dims))])
    return loudness


def noise(rng, shape, width, limit, cuts=(), kind=jnp.bfloat16):
    values = jax.random.normal(rng, shape, jnp.float32) * width
    if len(cuts) > 0:
        values = level_of(rng, shape, cuts, -0.22, 0.18) * values
    return jnp.clip(values, min=-limit, max=limit).astype(kind)


def setup_inputs(seed: int = 0) -> dict:
    splits = jax.random.split(jax.random.key(seed), 8)
    queries = draw_queries(jax.random.fold_in(splits[7], 71), 0)
    keys = draw_keys(jax.random.fold_in(splits[7], 71), 0)
    values = noise(splits[2], (TOKENS, D), 1.0, 6.0, ((0, 128), (1, 4)))
    out_weight = noise(splits[3], (D, D), D ** -0.5, 0.1875, ((0, 4),))
    out_grad = noise(splits[4], (TOKENS, D), 1.0, 6.0, ((0, 128), (1, 4)))
    near_offsets = draw_near_offsets(jax.random.fold_in(splits[7], 71), 0)
    coupling = place_ends(jax.random.randint(splits[6], (NBLK, C1), 0, NSUP), jax.random.fold_in(splits[6], 1), 0, NSUP - 1).astype(jnp.int32)
    return {"queries": queries, "keys": keys, "values": values, "out_weight": out_weight, "out_grad": out_grad, "near_offsets": near_offsets, "coupling": coupling}


def rounded(array):
    return lax.optimization_barrier(array.astype(jnp.bfloat16)).astype(jnp.float32)

def reference(queries, keys, values, out_weight, out_grad, near_offsets, coupling):
    key_vals = jnp.concatenate([keys, values], 1)
    fine_rows = (lax.optimization_barrier(jnp.sum(key_vals.astype(jnp.float32).reshape(NBLK, NB, 2 * D), 1)) / math.sqrt(NB)).astype(jnp.bfloat16)
    top_rows = (lax.optimization_barrier(jnp.sum(fine_rows.astype(jnp.float32).reshape(NSUP, GROUP, 2 * D), 1)) / math.sqrt(GROUP)).astype(jnp.bfloat16)
    padded = jnp.pad(key_vals.reshape(NBLK, NB, 2 * D), ((2, 2), (0, 0), (0, 0)))
    tile_rows = fine_rows.reshape(NSUP, GROUP, 2 * D)
    query_blks = queries.reshape(NBLK, NB, HEADS, HD)
    root_dim = math.sqrt(HD)

    def attend(block_id):
        shifts = near_offsets[block_id].astype(jnp.int32)
        near_rows = padded[block_id + shifts + 2].reshape(3 * NB, 2 * D)
        far_rows = tile_rows[coupling[block_id]].reshape(C1 * GROUP, 2 * D)
        all_rows = jnp.concatenate([near_rows, far_rows, top_rows], 0)
        target = block_id + shifts
        inside = (target >= 0) & (target < NBLK)
        usable = jnp.concatenate([jnp.repeat(inside, NB), jnp.ones((C1 * GROUP + NSUP,), bool)])
        keys_all = all_rows[:, :D].reshape(-1, HEADS, HD).astype(jnp.float32)
        vals_all = all_rows[:, D:].reshape(-1, HEADS, HD).astype(jnp.float32)
        query_blk = query_blks[block_id].astype(jnp.float32)
        scores = jnp.einsum('qhd,khd->hqk', query_blk, keys_all) / root_dim
        scores = jnp.where(usable[None, None, :], scores, -jnp.inf)
        row_peak = lax.optimization_barrier(jnp.max(scores, -1, keepdims=True))
        exp_scores = jnp.exp(scores - row_peak)
        attn_prob = exp_scores / lax.optimization_barrier(jnp.sum(exp_scores, -1, keepdims=True))
        return (attn_prob, keys_all, vals_all, query_blk, shifts)

    def forward(block_id):
        attn_prob, keys_all, vals_all, query_blk, shifts = attend(block_id)
        return jnp.einsum('hqk,khd->qhd', rounded(attn_prob), vals_all).astype(jnp.bfloat16)
    block_list = jnp.arange(NBLK).astype(jnp.int32)
    attended = lax.map(forward, block_list).reshape(TOKENS, D)
    mixed = jnp.dot(attended, out_weight, preferred_element_type=jnp.float32).astype(jnp.bfloat16)
    grad_attn = jnp.dot(out_grad, out_weight.T, preferred_element_type=jnp.float32).astype(jnp.bfloat16)
    grad_weight = jnp.dot(attended.T, out_grad, preferred_element_type=jnp.float32)
    grad_blks = grad_attn.reshape(NBLK, NB, HEADS, HD)
    near_count = 3 * NB
    far_count = C1 * GROUP

    def backward(state, block_id):
        grad_pad, grad_tiles, grad_top = state
        attn_prob, keys_all, vals_all, query_blk, shifts = attend(block_id)
        grad_out = grad_blks[block_id].astype(jnp.float32)
        dprob = jnp.einsum('qhd,khd->hqk', grad_out, vals_all)
        inner = lax.optimization_barrier(jnp.sum(attn_prob * dprob, -1, keepdims=True))
        dscore = rounded(attn_prob * (dprob - inner) / root_dim)
        grad_query = jnp.einsum('hqk,khd->qhd', dscore, keys_all).astype(jnp.bfloat16)
        grad_key = jnp.einsum('hqk,qhd->khd', dscore, query_blk).reshape(-1, D)
        grad_val = jnp.einsum('hqk,qhd->khd', rounded(attn_prob), grad_out).reshape(-1, D)
        grad_rows = jnp.concatenate([grad_key, grad_val], 1)
        grad_pad = grad_pad.at[block_id + shifts + 2].add(grad_rows[:near_count].reshape(3, NB, 2 * D))
        grad_tiles = grad_tiles.at[coupling[block_id]].add(grad_rows[near_count:near_count + far_count].reshape(C1, GROUP, 2 * D))
        grad_top = grad_top + grad_rows[near_count + far_count:]
        return ((grad_pad, grad_tiles, grad_top), grad_query)
    initial = (jnp.zeros((NBLK + 4, NB, 2 * D), jnp.float32), jnp.zeros((NSUP, GROUP, 2 * D), jnp.float32), jnp.zeros((NSUP, 2 * D), jnp.float32))
    (grad_pad, grad_tiles, grad_top), grad_queries = lax.scan(backward, initial, block_list)
    grad_fine = grad_tiles.reshape(NBLK, 2 * D) + jnp.repeat(grad_top / math.sqrt(GROUP), GROUP, axis=0)
    grad_tokens = (grad_pad[2:-2] + grad_fine[:, None, :] / math.sqrt(NB)).reshape(TOKENS, 2 * D)
    return (mixed, grad_queries.reshape(TOKENS, D), grad_tokens[:, :D].astype(jnp.bfloat16), grad_tokens[:, D:].astype(jnp.bfloat16), grad_weight)
```

```python
import functools

import jax
import jax.numpy as jnp
from jax import lax
from jax.experimental import pallas as pl
from jax.experimental.pallas import tpu as pltpu
from jax.sharding import PartitionSpec as P

MESH = pl.DeviceIdType.MESH
F32 = jnp.float32
BF16 = jnp.bfloat16
HD = 64
NB = 64
BLK = 4
HEADS = 4
COLS = HEADS * HD
TOK = BLK * NB
C1 = 16
LANE = 128
SUB = 16
NEAR = 5 * NB
FAR = C1 * BLK


def each(low, high, body):
    lax.fori_loop(low, high, lambda k, c: (body(k), c)[1], 0)


def dot_nn(a, b):
    return lax.dot_general(a, b, (((1,), (0,)), ((), ())), preferred_element_type=F32)


def dot_nt(a, b):
    return lax.dot_general(a, b, (((1,), (1,)), ((), ())), preferred_element_type=F32)


def dot_tn(a, b):
    return lax.dot_general(a, b, (((0,), (0,)), ((), ())), preferred_element_type=F32)


def iota(shape, dim):
    return lax.broadcasted_iota(jnp.int32, shape, dim)


class Place:
    def __init__(self, n, tps):
        self.n, self.tps = n, tps
        self.seqs = 2 * n * n
        self.seq = lax.axis_index("seq")
        self.tp = lax.axis_index("tp")
        self.z = lax.div(self.seq, 2 * n)
        self.y = lax.rem(lax.div(self.seq, 2), n)
        self.xh = lax.rem(self.seq, 2)
        self.mine = self.z * (1 - self.xh) + self.y * self.xh
        self.cross = self.y * (1 - self.xh) + self.z * self.xh
        self.spot = self.xh * n * n + self.cross * n + self.mine

    def at(self, z, y, xh):
        return (z * (2 * self.n) + y * 2 + xh, self.tp)

    def along_mine(self, k, xh):
        c = lax.rem(self.mine + k, self.n)
        return self.at(
            c * (1 - self.xh) + self.z * self.xh, self.y * (1 - self.xh) + c * self.xh, xh
        )

    def along_cross(self, k, xh):
        c = lax.rem(self.cross + k, self.n)
        return c, self.at(
            self.z * (1 - self.xh) + c * self.xh, c * (1 - self.xh) + self.y * self.xh, xh
        )

    def along_y(self, k):
        c = lax.rem(self.y + k, self.n)
        return c, self.at(self.z, c, self.xh)

    def along_z(self, k):
        c = lax.rem(self.z + k, self.n)
        return c, self.at(c, self.y, self.xh)

    def step(self, by):
        return (lax.rem(self.seq + self.seqs + by, self.seqs), self.tp)

    def tp_at(self, k):
        c = lax.rem(self.tp + k, self.tps)
        return c, (self.seq, c)


def remote(src, dst, send, recv, device):
    return pltpu.make_async_remote_copy(
        src_ref=src, dst_ref=dst, send_sem=send, recv_sem=recv, device_id=device, device_id_type=MESH
    )


def gather_1(w, buf, send, recv, act):
    def same(k):
        act(remote(buf.at[w.spot], buf.at[w.spot], send.at[0, k], recv.at[0, k], w.along_mine(k, w.xh)))

    def other(k):
        act(remote(buf.at[w.spot], buf.at[w.spot], send.at[1, k], recv.at[1, k], w.along_mine(k, 1 - w.xh)))

    each(1, w.n, same)
    each(0, w.n, other)


def gather_2(w, buf, send, recv, act):
    n = w.n

    def one(k):
        rows = buf.at[pl.ds(w.y * n, n)]
        act(remote(rows, rows, send.at[0, k], recv.at[0, k], w.along_y(k)[1]))
        rows = buf.at[pl.ds(n * n + w.z * n, n)]
        act(remote(rows, rows, send.at[1, k], recv.at[1, k], w.along_z(k)[1]))

    each(1, n, one)


def scatter_1(w, part, got, send, recv, act):
    n = w.n

    def one(k):
        c, device = w.along_y(k)
        act(remote(part.at[pl.ds(c * n, n)], got.at[0, k], send.at[0, k], recv.at[0, k], device))
        c, device = w.along_z(k)
        act(remote(part.at[pl.ds(n * n + c * n, n)], got.at[1, k], send.at[1, k], recv.at[1, k], device))

    each(1, n, one)


def reduce_1(w, part, got, rows):
    n = w.n
    for half, row in ((0, w.y), (1, w.z)):
        total = part[pl.ds(half * n * n + row * n, n)].astype(F32)
        for k in range(1, n):
            total += got[half, k].astype(F32)
        rows[half] = total.astype(BF16)


def scatter_2(w, rows, got, send, recv, act):
    def same(k):
        c = lax.rem(w.mine + k, w.n)
        act(remote(rows.at[w.xh, c], got.at[0, k], send.at[0, k], recv.at[0, k], w.along_mine(k, w.xh)))

    def other(k):
        c, device = w.along_cross(k, 1 - w.xh)
        act(remote(rows.at[1 - w.xh, c], got.at[1, k], send.at[1, k], recv.at[1, k], device))

    each(1, w.n, same)
    each(0, w.n, other)


def reduce_2(w, rows, got):
    total = rows[w.xh, w.mine].astype(F32)
    for k in range(1, w.n):
        total += got[0, k].astype(F32)
    for k in range(w.n):
        total += got[1, k].astype(F32)
    return total


def start(copy):
    copy.start()


def landed(copy):
    copy.wait_recv()


def sent(copy):
    copy.wait_send()


def kernel(
    n, tps, group,
    off_ref, cpl_ref, q_ref, k_ref, v_ref, w_ref, og_ref,
    mixed_ref, gq_ref, gk_ref, gv_ref, gw_ref,
    kpad, vpad, fine, ogs, kft, vft, hot, probs, halves, att, gatt, mine_out,
    msend, mgot, gkpad, gvpad, hsend, hgot, dlist, dtop,
    wpart, wgot1, wrows, wgot2, wfull, fpart, fgot1, frows, fgot2,
    s_g1, r_g1, s_g2, r_g2, s_h, r_h, s_o, r_o, s_m, r_m, s_b, r_b,
    s_w1, r_w1, s_w2, r_w2, s_w3, r_w3, s_w4, r_w4, s_f1, r_f1, s_f2, r_f2,
):
    w = Place(n, tps)
    tiles = w.seqs
    groups = tiles // group
    nblk = tiles * BLK

    barrier = pltpu.get_barrier_semaphore()

    def greet(device):
        pl.semaphore_signal(barrier, inc=1, device_id=device, device_id_type=MESH)

    def greet_square(k):
        greet(w.along_y(k)[1])
        greet(w.along_z(k)[1])
        greet(w.along_mine(k, 1 - w.xh))
        greet(w.along_cross(k, 1 - w.xh)[1])

    each(1, n, greet_square)
    greet(w.at(w.z, w.y, 1 - w.xh))
    greet(w.step(1))
    greet(w.step(-1))
    each(1, tps, lambda k: greet(w.tp_at(k)[1]))

    piece = jnp.zeros((SUB, LANE), F32)
    for c in range(4):
        row, tok = iota((SUB, TOK), 0), iota((SUB, TOK), 1)
        pick = jnp.where((row - c * BLK) == (tok >> 6), 1.0, 0.0).astype(BF16)
        src = k_ref if c < 2 else v_ref
        piece += dot_nn(pick, src[:, (c % 2) * LANE : (c % 2 + 1) * LANE])
    fine[w.spot] = (piece * 0.125).astype(BF16)
    ogs[w.tp] = og_ref[...]
    pl.semaphore_wait(barrier, 4 * (n - 1) + 3 + tps - 1)

    half = TOK // 2

    def halo(act):
        for i, (src, pad) in enumerate(((k_ref, kpad), (v_ref, vpad))):
            act(remote(src.at[pl.ds(half, half)], pad.at[pl.ds(0, half)], s_h.at[i], r_h.at[i], w.step(1)))
            act(remote(src.at[pl.ds(0, half)], pad.at[pl.ds(half + TOK, half)], s_h.at[2 + i], r_h.at[2 + i], w.step(-1)))

    def columns(act):
        def one(k):
            act(remote(og_ref, ogs.at[w.tp], s_o.at[k], r_o.at[k], w.tp_at(k)[1]))

        each(1, tps, one)

    gather_1(w, fine, s_g1, r_g1, start)
    halo(start)
    columns(start)

    kpad[half : half + TOK] = k_ref[...]
    vpad[half : half + TOK] = v_ref[...]
    gkpad[...] = jnp.zeros_like(gkpad)
    gvpad[...] = jnp.zeros_like(gvpad)
    dtop[...] = jnp.zeros_like(dtop)

    spot = iota((1, tiles), 1)
    in_square, bits = spot & (n * n - 1), n.bit_length() - 1
    a, c = in_square >> bits, in_square & (n - 1)
    tile_of = jnp.where(spot < n * n, c * (2 * n) + a * 2, a * (2 * n) + c * 2 + 1)
    rows8 = iota((8, tiles), 0)
    listed = []
    for g in range(BLK * C1 // 8):
        wanted = jnp.zeros((8, tiles), jnp.int32)
        for i in range(8):
            at = g * 8 + i
            wanted = jnp.where(rows8 == i, cpl_ref[at // C1, at % C1], wanted)
        listed.append(wanted)
    wanted = jnp.concatenate(listed, 0)
    hot[...] = jnp.where(wanted == tile_of, 1.0, 0.0).astype(BF16)

    size = group * SUB
    to, fro = iota((size, size), 0), iota((size, size), 1)
    gbits = group.bit_length() - 1
    swapped = (fro & (SUB - 1)) * group + (fro >> 4)
    swap = jnp.where(to == swapped, 1.0, 0.0).astype(BF16)
    swapped = (fro & (group - 1)) * SUB + (fro >> gbits)
    swap_back = jnp.where(to == swapped, 1.0, 0.0).astype(BF16)

    head_of = iota((1, COLS), 1) >> 6
    masks = [jnp.where(head_of == h, 1.0, 0.0) for h in range(HEADS)]
    masks_b = [m.astype(BF16) for m in masks]

    def diagonal(rows):
        return jnp.concatenate([rows * m for m in masks_b], 0)

    def collect(full):
        out = full[0:NB] * masks[0]
        for h in range(1, HEADS):
            out += full[h * NB : (h + 1) * NB] * masks[h]
        return out

    gather_1(w, fine, s_g1, r_g1, landed)
    gather_2(w, fine, s_g2, r_g2, start)
    halo(landed)
    gather_2(w, fine, s_g2, r_g2, landed)

    packed = jnp.concatenate([fine[g * group : (g + 1) * group].reshape(size, LANE) for g in range(groups)], 1)
    by_row = dot_nn(swap, packed)
    flat = jnp.concatenate(
        [
            jnp.concatenate([by_row[s * group : (s + 1) * group, g * LANE : (g + 1) * LANE] for s in range(SUB)], 1)
            for g in range(groups)
        ],
        0,
    )
    tops = []
    for c in range(4):
        total = flat[:, c * BLK * LANE : (c * BLK + 1) * LANE]
        for r in range(1, BLK):
            total += flat[:, (c * BLK + r) * LANE : (c * BLK + r + 1) * LANE]
        tops.append((total * 0.5).astype(BF16))
    far = dot_nn(hot[...], flat.astype(BF16)).astype(BF16)
    for b in range(BLK):
        for r in range(BLK):
            for c in range(4):
                s = c * BLK + r
                into = kft if c < 2 else vft
                into[b, r * C1 : (r + 1) * C1, (c % 2) * LANE : (c % 2 + 1) * LANE] = far[
                    b * C1 : (b + 1) * C1, s * LANE : (s + 1) * LANE
                ]
        kft[b, FAR:, :LANE], kft[b, FAR:, LANE:] = tops[0], tops[1]
        vft[b, FAR:, :LANE], vft[b, FAR:, LANE:] = tops[2], tops[3]

    def listed_rows(pad, rest, b):
        return jnp.concatenate([pad[b * NB : b * NB + NEAR], rest[b]], 0)

    for b in range(BLK):
        keys = listed_rows(kpad, kft, b)
        vals = listed_rows(vpad, vft, b)
        scores = dot_nt(keys, diagonal(q_ref[b * NB : (b + 1) * NB])) * 0.125
        parts = []
        for d in range(5):
            target = w.seq * BLK + b + d - 2
            chosen = (off_ref[b, 0] == d - 2) | (off_ref[b, 1] == d - 2) | (off_ref[b, 2] == d - 2)
            usable = chosen & (target >= 0) & (target < nblk)
            parts.append(scores[d * NB : (d + 1) * NB] + jnp.where(usable, 0.0, -1e30))
        scores = jnp.concatenate(parts + [scores[NEAR:]], 0)
        peak = jnp.max(scores, 0, keepdims=True)
        exps = jnp.exp(scores - peak)
        prob = exps * (1.0 / jnp.sum(exps, 0, keepdims=True))
        prob_b = prob.astype(BF16)
        probs[b] = prob
        halves[b] = prob_b
        att[b * NB : (b + 1) * NB] = collect(dot_tn(prob_b, vals)).astype(BF16)

    columns(landed)
    for t in range(tps):
        part = dot_tn(att[...], ogs[t]).astype(BF16)
        for j in range(COLS // LANE):
            wpart[(t * 2 + j) * 16 : (t * 2 + j + 1) * 16] = part[:, j * LANE : (j + 1) * LANE].reshape(16, SUB, LANE)
    scatter_1(w, wpart, wgot1, s_w1, r_w1, start)

    for t in range(tps):
        msend[t] = dot_nn(att[...], w_ref[:, t * COLS : (t + 1) * COLS]).astype(BF16)

    def mix(act):
        def one(k):
            c, device = w.tp_at(k)
            act(remote(msend.at[c], mgot.at[k], s_m.at[k], r_m.at[k], device))

        each(1, tps, one)

    mix(start)
    mine_out[...] = dot_nn(att[...], w_ref[:, pl.ds(pl.multiple_of(w.tp * COLS, COLS), COLS)])

    grad = dot_nt(ogs[0], w_ref[:, 0:COLS])
    for t in range(1, tps):
        grad += dot_nt(ogs[t], w_ref[:, t * COLS : (t + 1) * COLS])
    gatt[...] = grad.astype(BF16)

    for b in range(BLK):
        keys = listed_rows(kpad, kft, b)
        vals = listed_rows(vpad, vft, b)
        q_diag = diagonal(q_ref[b * NB : (b + 1) * NB])
        g_diag = diagonal(gatt[b * NB : (b + 1) * NB])
        prob = probs[b]
        dprob = dot_nt(vals, g_diag)
        inner = jnp.sum(prob * dprob, 0, keepdims=True)
        dscore = (prob * (dprob - inner) * 0.125).astype(BF16)
        gq_ref[b * NB : (b + 1) * NB] = collect(dot_tn(dscore, keys)).astype(BF16)
        dkey = dot_nn(dscore, q_diag)
        dval = dot_nn(halves[b], g_diag)
        gkpad[b * NB : b * NB + NEAR] += dkey[:NEAR]
        gvpad[b * NB : b * NB + NEAR] += dval[:NEAR]
        for r in range(BLK):
            for c in range(4):
                s = c * BLK + r
                src = dkey if c < 2 else dval
                dlist[b * C1 : (b + 1) * C1, s * LANE : (s + 1) * LANE] = src[
                    NEAR + r * C1 : NEAR + (r + 1) * C1, (c % 2) * LANE : (c % 2 + 1) * LANE
                ].astype(BF16)
        dtop[:, :COLS] += dkey[NEAR + FAR :]
        dtop[:, COLS:] += dval[NEAR + FAR :]

    for i, pad in enumerate((gkpad, gvpad)):
        hsend[i] = pad[half + TOK :].astype(BF16)
        hsend[2 + i] = pad[:half].astype(BF16)

    def halo_back(act):
        for i in range(2):
            act(remote(hsend.at[i], hgot.at[i], s_b.at[i], r_b.at[i], w.step(1)))
            act(remote(hsend.at[2 + i], hgot.at[2 + i], s_b.at[2 + i], r_b.at[2 + i], w.step(-1)))

    tile_grad = dot_tn(hot[...], dlist[...])
    cols = []
    for c in range(4):
        for r in range(BLK):
            s = c * BLK + r
            cols.append(tile_grad[:, s * LANE : (s + 1) * LANE] + dtop[:, c * LANE : (c + 1) * LANE] * 0.5)
    by_row = jnp.concatenate(
        [
            jnp.concatenate([cols[s][g * group : (g + 1) * group] for s in range(SUB)], 0)
            for g in range(groups)
        ],
        1,
    ).astype(BF16)
    packed = dot_nn(swap_back, by_row).astype(BF16)
    for g in range(groups):
        fpart[g * group : (g + 1) * group] = packed[:, g * LANE : (g + 1) * LANE].reshape(group, SUB, LANE)
    scatter_1(w, fpart, fgot1, s_f1, r_f1, start)
    halo_back(start)

    scatter_1(w, wpart, wgot1, s_w1, r_w1, landed)
    reduce_1(w, wpart, wgot1, wrows)
    scatter_2(w, wrows, wgot2, s_w2, r_w2, start)

    scatter_1(w, fpart, fgot1, s_f1, r_f1, landed)
    reduce_1(w, fpart, fgot1, frows)
    scatter_2(w, frows, fgot2, s_f2, r_f2, start)

    scatter_2(w, wrows, wgot2, s_w2, r_w2, landed)
    wfull[w.spot] = reduce_2(w, wrows, wgot2).astype(BF16)
    gather_1(w, wfull, s_w3, r_w3, start)

    mix(landed)
    total = mine_out[...]
    for k in range(1, tps):
        total += mgot[k].astype(F32)
    mixed_ref[...] = total.astype(BF16)
    halo_back(landed)

    gather_1(w, wfull, s_w3, r_w3, landed)
    gather_2(w, wfull, s_w4, r_w4, start)

    scatter_2(w, frows, fgot2, s_f2, r_f2, landed)
    fine_grad = reduce_2(w, frows, fgot2) * 0.125
    for i, (pad, out) in enumerate(((gkpad, gk_ref), (gvpad, gv_ref))):
        for r in range(BLK):
            rows = pad[half + r * NB : half + (r + 1) * NB]
            if r < BLK // 2:
                rows += hgot[i, r * NB : (r + 1) * NB].astype(F32)
            else:
                rows += hgot[2 + i, r * NB - half : (r + 1) * NB - half].astype(F32)
            for c in range(2):
                s = (2 * i + c) * BLK + r
                out[r * NB : (r + 1) * NB, c * LANE : (c + 1) * LANE] = (
                    rows[:, c * LANE : (c + 1) * LANE] + fine_grad[s : s + 1]
                ).astype(BF16)

    gather_2(w, wfull, s_w4, r_w4, landed)
    for j in range(tps * COLS // LANE):
        gw_ref[:, j * LANE : (j + 1) * LANE] = wfull[j * 16 : (j + 1) * 16].reshape(COLS, LANE).astype(F32)

    gather_1(w, fine, s_g1, r_g1, sent)
    gather_2(w, fine, s_g2, r_g2, sent)
    halo(sent)
    columns(sent)
    scatter_1(w, wpart, wgot1, s_w1, r_w1, sent)
    mix(sent)
    halo_back(sent)
    scatter_1(w, fpart, fgot1, s_f1, r_f1, sent)
    scatter_2(w, wrows, wgot2, s_w2, r_w2, sent)
    scatter_2(w, frows, fgot2, s_f2, r_f2, sent)
    gather_1(w, wfull, s_w3, r_w3, sent)
    gather_2(w, wfull, s_w4, r_w4, sent)


def shards(n, tps, queries, keys, values, out_weight, out_grad, near_offsets, coupling):
    tiles = 2 * n * n
    group = min(16, tiles)
    pieces = (tiles, SUB, LANE)
    dma = lambda *shape: pltpu.SemaphoreType.DMA(shape)
    vm = lambda dtype, *shape: pltpu.VMEM(shape, dtype)
    pair = [dma(2, n), dma(2, n)]
    in_vmem = pl.BlockSpec(memory_space=pltpu.VMEM)
    in_smem = pl.BlockSpec(memory_space=pltpu.SMEM)
    rest = FAR + tiles
    length = NEAR + rest
    sums = [vm(BF16, *pieces), vm(BF16, 2, n, n, SUB, LANE), vm(BF16, 2, n, SUB, LANE), vm(BF16, 2, n, SUB, LANE)]
    scratch = [
        vm(BF16, 2 * TOK, COLS), vm(BF16, 2 * TOK, COLS), vm(BF16, *pieces), vm(BF16, tps, TOK, COLS),
        vm(BF16, BLK, rest, COLS), vm(BF16, BLK, rest, COLS), vm(BF16, BLK * C1, tiles),
        vm(F32, BLK, length, COLS), vm(BF16, BLK, length, COLS), vm(BF16, TOK, COLS), vm(BF16, TOK, COLS), vm(F32, TOK, COLS),
        vm(BF16, tps, TOK, COLS), vm(BF16, tps, TOK, COLS), vm(F32, 2 * TOK, COLS), vm(F32, 2 * TOK, COLS),
        vm(BF16, 4, TOK // 2, COLS), vm(BF16, 4, TOK // 2, COLS), vm(BF16, BLK * C1, SUB * LANE), vm(F32, tiles, 2 * COLS),
        *sums, vm(BF16, *pieces), *sums,
        *pair, *pair, dma(4), dma(4), dma(tps), dma(tps), dma(tps), dma(tps), dma(4), dma(4),
        *pair, *pair, *pair, *pair, *pair, *pair,
    ]
    like = lambda x: jax.ShapeDtypeStruct(x.shape, BF16)
    return pl.pallas_call(
        functools.partial(kernel, n, tps, group),
        out_shape=(
            like(out_grad), like(queries), like(keys), like(values),
            jax.ShapeDtypeStruct(out_weight.shape, F32),
        ),
        in_specs=[in_smem] * 2 + [in_vmem] * 5,
        out_specs=[in_vmem] * 5,
        scratch_shapes=scratch,
        compiler_params=pltpu.CompilerParams(
            collective_id=0, has_side_effects=True, vmem_limit_bytes=48 * 1024 * 1024
        ),
    )(near_offsets, coupling, queries, keys, values, out_weight, out_grad)


def solution(mesh):
    n = int(round((mesh.shape["seq"] // 2) ** 0.5))
    step = functools.partial(shards, n, mesh.shape["tp"])
    in_specs = (
        P("seq", "tp"),
        P("seq", "tp"),
        P("seq", "tp"),
        P("tp", None),
        P("seq", "tp"),
        P("seq", None),
        P("seq", None),
    )
    out_specs = (P("seq", "tp"), P("seq", "tp"), P("seq", "tp"), P("seq", "tp"), P("tp", None))
    return jax.shard_map(step, mesh=mesh, in_specs=in_specs, out_specs=out_specs, check_vma=False)
```

```python
import functools

import jax
import jax.numpy as jnp
from jax import lax
from jax.experimental import pallas as pl
from jax.experimental.pallas import tpu as pltpu
from jax.sharding import PartitionSpec as P

MESH = pl.DeviceIdType.MESH
F32 = jnp.float32
BF16 = jnp.bfloat16
HD = 64
NB = 64
BLK = 4
HEADS = 4
COLS = HEADS * HD
TOK = BLK * NB
C1 = 16
LANE = 128
SUB = 16
NEAR = 5 * NB
FAR = C1 * BLK
VMEM = 62 * 1024 * 1024


def each(low, high, body):
    lax.fori_loop(low, high, lambda k, c: (body(k), c)[1], 0)


def dot_nn(a, b):
    return lax.dot_general(a, b, (((1,), (0,)), ((), ())), preferred_element_type=F32)


def dot_nt(a, b):
    return lax.dot_general(a, b, (((1,), (1,)), ((), ())), preferred_element_type=F32)


def dot_tn(a, b):
    return lax.dot_general(a, b, (((0,), (0,)), ((), ())), preferred_element_type=F32)


def iota(shape, dim):
    return lax.broadcasted_iota(jnp.int32, shape, dim)


class Place:
    def __init__(self, n, tps):
        self.n, self.tps = n, tps
        self.seqs = 2 * n * n
        self.seq = lax.axis_index("seq")
        self.tp = lax.axis_index("tp")
        self.z = lax.div(self.seq, 2 * n)
        self.y = lax.rem(lax.div(self.seq, 2), n)
        self.xh = lax.rem(self.seq, 2)
        self.mine = self.z * (1 - self.xh) + self.y * self.xh
        self.cross = self.y * (1 - self.xh) + self.z * self.xh

    def by(self, slot):
        odd = lax.rem(slot, 2)
        return odd * lax.div(slot + 1, 2) + (1 - odd) * (self.n - lax.div(slot, 2))

    def back(self, slot):
        return slot + 2 * lax.rem(slot, 2) - 1 - lax.div(slot, self.n - 1)

    def slot(self, ahead):
        n = self.n
        upper = lax.div(n - 1 + n // 2 - ahead, n - 1)
        return upper * (2 * ahead - 1) + (1 - upper) * 2 * (n - ahead) + lax.div(n - 1 - ahead, n - 1)

    def at(self, z, y, xh):
        return (z * (2 * self.n) + y * 2 + xh, self.tp)

    def along_mine(self, slot, xh):
        c = lax.rem(self.mine + self.by(slot), self.n)
        return self.at(c * (1 - self.xh) + self.z * self.xh, self.y * (1 - self.xh) + c * self.xh, xh)

    def along_cross(self, slot, xh):
        c = lax.rem(self.cross + self.by(slot), self.n)
        return self.at(self.z * (1 - self.xh) + c * self.xh, c * (1 - self.xh) + self.y * self.xh, xh)

    def along_y(self, slot):
        return self.at(self.z, lax.rem(self.y + self.by(slot), self.n), self.xh)

    def along_z(self, slot):
        return self.at(lax.rem(self.z + self.by(slot), self.n), self.y, self.xh)

    def step(self, by):
        return (lax.rem(self.seq + self.seqs + by, self.seqs), self.tp)

    def tp_at(self, k):
        c = lax.rem(self.tp + k, self.tps)
        return c, (self.seq, c)

    def spots(self):
        n = self.n
        of_y = [self.slot(lax.rem(c + n - self.y, n)) for c in range(n)]
        of_z = [self.slot(lax.rem(c + n - self.z, n)) for c in range(n)]
        return [
            h * n * n + (of_z if h else of_y)[r] * n + (of_y if h else of_z)[c]
            for h in range(2)
            for r in range(n)
            for c in range(n)
        ]


def remote(src, dst, send, recv, device):
    return pltpu.make_async_remote_copy(
        src_ref=src, dst_ref=dst, send_sem=send, recv_sem=recv, device_id=device, device_id_type=MESH
    )


class Flight:
    def __init__(self, log, move, *args):
        self.move, self.args = move, args
        log.append(self)

    def begin(self):
        self.move(*self.args, lambda copy: copy.start())

    def land(self):
        self.move(*self.args, lambda copy: copy.wait_recv())

    def end(self):
        self.move(*self.args, lambda copy: copy.wait_send())


def spread(w, buf, send, recv, other, low, high, act):
    own = buf.at[w.xh * w.n * w.n]

    def one(i):
        into = buf.at[w.xh * w.n * w.n + w.back(i)]
        xh = 1 - w.xh if other else w.xh
        act(remote(own, into, send.at[other, i], recv.at[other, w.back(i)], w.along_mine(i, xh)))

    if low == 0:
        if other:
            act(remote(own, own, send.at[1, 0], recv.at[1, 0], w.at(w.z, w.y, 1 - w.xh)))
        low = 1
    each(low, high, one)


def relay(w, buf, send, recv, batch, other, low, high, act):
    n = w.n
    base = (1 - w.xh if other else w.xh) * n * n

    def one(i):
        j = w.back(i)
        mine = buf.at[pl.ds(base + low, high - low)]
        into = buf.at[pl.ds(base + j * n + low, high - low)]
        device = (w.along_mine if other else w.along_cross)(i, w.xh)
        act(remote(mine, into, send.at[batch, i], recv.at[batch, j], device))

    each(1, n, one)


class Gather:
    def __init__(self, log, w, buf, s_1, r_1, s_2, r_2):
        n = w.n
        cuts = [c for c in (1, 3, 5, 8) if c < n] + [n]
        same = list(zip([0] + cuts[:-1], cuts))
        cross = [(0, cuts[1])] + same[2:]
        self.out = [Flight(log, spread, w, buf, s_1, r_1, 1, 0, n), Flight(log, spread, w, buf, s_1, r_1, 0, 0, n)]
        steps = [(0, *part) for part in same] + [(1, *part) for part in cross]
        steps.sort(key=lambda step: (step[1] + 2 * step[0], step[0]))
        self.arrive = [Flight([], spread, w, buf, s_1, r_1, *step) for step in steps]
        self.onward = [Flight(log, relay, w, buf, s_2, r_2, i, *step) for i, step in enumerate(steps)]

    def begin(self):
        self.out[1].begin()
        self.out[0].begin()
        self.onward[0].begin()

    def forward(self):
        for arrived, onward in zip(self.arrive[1:], self.onward[1:]):
            arrived.land()
            onward.begin()

    def land(self):
        for onward in self.onward:
            onward.land()


def to_rows(w, part, got, send, recv, batch, low, high, act):
    n = w.n

    def one(i):
        for h, device in ((0, w.along_y(i)), (1, w.along_z(i))):
            mine = part.at[pl.ds(h * n * n + i * n + low, high - low)]
            act(remote(mine, got.at[h, i, pl.ds(low, high - low)], send.at[batch, h, i], recv.at[batch, h, i], device))

    each(1, n, one)


def to_owners(w, rows, got, send, recv, low, high, act):
    def same(i):
        act(remote(rows.at[w.xh, i], got.at[0, i], send.at[0, i], recv.at[0, i], w.along_mine(i, w.xh)))

    def other(i):
        act(remote(rows.at[1 - w.xh, i], got.at[1, i], send.at[1, i], recv.at[1, i], w.along_cross(i, 1 - w.xh)))

    each(max(low, 1), high, same)
    if low == 0:
        act(remote(rows.at[1 - w.xh, 0], got.at[1, 0], send.at[1, 0], recv.at[1, 0], w.at(w.z, w.y, 1 - w.xh)))
    each(max(low, 1), high, other)


class Scatter:
    def __init__(self, log, w, part, got_1, rows, got_2, s_1, r_1, s_2, r_2, cut):
        n = w.n
        self.w, self.part, self.got_1, self.rows, self.got_2 = w, part, got_1, rows, got_2
        self.cols = [(cut, n), (0, cut)] if cut else [(0, n)]
        self.first = [Flight(log, to_rows, w, part, got_1, s_1, r_1, i, *c) for i, c in enumerate(self.cols)]
        self.second = [Flight(log, to_owners, w, rows, got_2, s_2, r_2, *c) for c in self.cols]

    def begin(self):
        for first in self.first:
            first.begin()

    def forward(self):
        n = self.w.n
        for (low, high), first, second in zip(self.cols, self.first, self.second):
            first.land()
            for h in range(2):
                total = self.part[h * n * n + low : h * n * n + high].astype(F32)
                for i in range(1, n):
                    total += self.got_1[h, i, low:high].astype(F32)
                self.rows[h, low:high] = total.astype(BF16)
            second.begin()

    def land(self):
        for second in self.second:
            second.land()
        total = self.rows[self.w.xh, 0].astype(F32)
        for i in range(1, self.w.n):
            total += self.got_2[0, i].astype(F32)
        for i in range(self.w.n):
            total += self.got_2[1, i].astype(F32)
        return total


def kernel(
    n, tps, group,
    off_in, cpl_in, q_in, k_in, v_in, w_in, og_in,
    mixed_out, gq_out, gk_out, gv_out, pieces_out,
    off_ref, cpl_ref, q_ref, k_ref, v_ref, w_ref, og_ref, s_in,
    mixed_ref, gq_ref, gk_ref, gv_ref, s_out,
    kpad, vpad, fine, ogs, kft, vft, hot, probs, halves, att, gatt, mine_out,
    msend, mgot, gkpad, gvpad, hsend, hgot, dlist, dtop,
    wpart, wgot1, wrows, wgot2, wfull, fpart, fgot1, frows, fgot2,
    s_h, r_h, s_o, r_o, s_m, r_m, s_b, r_b,
    s_g1, r_g1, s_g2, r_g2, s_w1, r_w1, s_w2, r_w2, s_w3, r_w3, s_w4, r_w4, s_f1, r_f1, s_f2, r_f2,
):
    w = Place(n, tps)
    tiles = w.seqs
    groups = tiles // group
    nblk = tiles * BLK
    half = TOK // 2
    flights = []

    brought = [
        pltpu.make_async_copy(src, dst, s_in.at[i])
        for i, (src, dst) in enumerate(
            ((k_in, k_ref), (v_in, v_ref), (og_in, og_ref), (cpl_in, cpl_ref), (off_in, off_ref), (q_in, q_ref), (w_in, w_ref))
        )
    ]
    for copy in brought:
        copy.start()

    barrier = pltpu.get_barrier_semaphore()

    def greet(device):
        pl.semaphore_signal(barrier, inc=1, device_id=device, device_id_type=MESH)

    def greet_square(i):
        greet(w.along_y(i))
        greet(w.along_z(i))
        greet(w.along_mine(i, 1 - w.xh))
        greet(w.along_cross(i, 1 - w.xh))

    each(1, n, greet_square)
    greet(w.at(w.z, w.y, 1 - w.xh))
    greet(w.step(1))
    greet(w.step(-1))
    each(1, tps, lambda k: greet(w.tp_at(k)[1]))

    for copy in brought[:2]:
        copy.wait()
    piece = jnp.zeros((SUB, LANE), F32)
    for c in range(4):
        row, tok = iota((SUB, TOK), 0), iota((SUB, TOK), 1)
        pick = jnp.where((row - c * BLK) == (tok >> 6), 1.0, 0.0).astype(BF16)
        src = k_ref if c < 2 else v_ref
        piece += dot_nn(pick, src[:, (c % 2) * LANE : (c % 2 + 1) * LANE])
    fine[w.xh * n * n] = (piece * 0.125).astype(BF16)
    pl.semaphore_wait(barrier, 4 * (n - 1) + 3 + tps - 1)

    def move_halo(act):
        for i, (src, pad) in enumerate(((k_ref, kpad), (v_ref, vpad))):
            act(remote(src.at[pl.ds(half, half)], pad.at[pl.ds(0, half)], s_h.at[i], r_h.at[i], w.step(1)))
            act(remote(src.at[pl.ds(0, half)], pad.at[pl.ds(half + TOK, half)], s_h.at[2 + i], r_h.at[2 + i], w.step(-1)))

    def move_columns(act):
        def one(k):
            act(remote(og_ref, ogs.at[w.tp], s_o.at[k], r_o.at[k], w.tp_at(k)[1]))

        each(1, tps, one)

    summaries = Gather(flights, w, fine, s_g1, r_g1, s_g2, r_g2)
    halo = Flight(flights, move_halo)
    columns = Flight(flights, move_columns)
    summaries.begin()
    halo.begin()
    brought[2].wait()
    columns.begin()

    ogs[w.tp] = og_ref[...]
    kpad[half : half + TOK] = k_ref[...]
    vpad[half : half + TOK] = v_ref[...]
    gkpad[...] = jnp.zeros_like(gkpad)
    gvpad[...] = jnp.zeros_like(gvpad)
    dtop[...] = jnp.zeros_like(dtop)
    for copy in brought[3:]:
        copy.wait()

    bits = n.bit_length() - 1
    place = iota((1, tiles), 1)

    def ahead(slot):
        return jnp.where((slot & 1) == 1, (slot + 1) >> 1, n - (slot >> 1))

    by_row, by_col = ahead((place >> bits) & (n - 1)), ahead(place & (n - 1))
    tile_of = jnp.where(
        place < n * n,
        ((w.z + by_col) & (n - 1)) * (2 * n) + ((w.y + by_row) & (n - 1)) * 2,
        ((w.z + by_row) & (n - 1)) * (2 * n) + ((w.y + by_col) & (n - 1)) * 2 + 1,
    )
    rows8 = iota((8, tiles), 0)
    listed = []
    for g in range(BLK * C1 // 8):
        wanted = jnp.zeros((8, tiles), jnp.int32)
        for i in range(8):
            at = g * 8 + i
            wanted = jnp.where(rows8 == i, cpl_ref[at // C1, at % C1], wanted)
        listed.append(wanted)
    wanted = jnp.concatenate(listed, 0)
    hot[...] = jnp.where(wanted == tile_of, 1.0, 0.0).astype(BF16)

    size = group * SUB
    to, fro = iota((size, size), 0), iota((size, size), 1)
    gbits = group.bit_length() - 1
    swapped = (fro & (SUB - 1)) * group + (fro >> 4)
    swap = jnp.where(to == swapped, 1.0, 0.0).astype(BF16)
    swapped = (fro & (group - 1)) * SUB + (fro >> gbits)
    swap_back = jnp.where(to == swapped, 1.0, 0.0).astype(BF16)

    head_of = iota((1, COLS), 1) >> 6
    masks = [jnp.where(head_of == h, 1.0, 0.0) for h in range(HEADS)]
    masks_b = [m.astype(BF16) for m in masks]

    def diagonal(rows):
        return jnp.concatenate([rows * m for m in masks_b], 0)

    def collect(full):
        out = full[0:NB] * masks[0]
        for h in range(1, HEADS):
            out += full[h * NB : (h + 1) * NB] * masks[h]
        return out

    summaries.forward()

    columns.land()
    grad = dot_nt(ogs[0], w_ref[:, 0:COLS])
    for t in range(1, tps):
        grad += dot_nt(ogs[t], w_ref[:, t * COLS : (t + 1) * COLS])
    gatt[...] = grad.astype(BF16)
    spots = w.spots()

    halo.land()
    summaries.land()

    packed = jnp.concatenate([fine[g * group : (g + 1) * group].reshape(size, LANE) for g in range(groups)], 1)
    by_row = dot_nn(swap, packed)
    flat = jnp.concatenate(
        [
            jnp.concatenate([by_row[s * group : (s + 1) * group, g * LANE : (g + 1) * LANE] for s in range(SUB)], 1)
            for g in range(groups)
        ],
        0,
    )
    tops = []
    for c in range(4):
        total = flat[:, c * BLK * LANE : (c * BLK + 1) * LANE]
        for r in range(1, BLK):
            total += flat[:, (c * BLK + r) * LANE : (c * BLK + r + 1) * LANE]
        tops.append((total * 0.5).astype(BF16))
    far = dot_nn(hot[...], flat.astype(BF16)).astype(BF16)
    for b in range(BLK):
        for r in range(BLK):
            for c in range(4):
                s = c * BLK + r
                into = kft if c < 2 else vft
                into[b, r * C1 : (r + 1) * C1, (c % 2) * LANE : (c % 2 + 1) * LANE] = far[
                    b * C1 : (b + 1) * C1, s * LANE : (s + 1) * LANE
                ]
        kft[b, FAR:, :LANE], kft[b, FAR:, LANE:] = tops[0], tops[1]
        vft[b, FAR:, :LANE], vft[b, FAR:, LANE:] = tops[2], tops[3]

    def listed_rows(pad, rest, b):
        return jnp.concatenate([pad[b * NB : b * NB + NEAR], rest[b]], 0)

    for b in range(BLK):
        keys = listed_rows(kpad, kft, b)
        vals = listed_rows(vpad, vft, b)
        scores = dot_nt(keys, diagonal(q_ref[b * NB : (b + 1) * NB])) * 0.125
        parts = []
        for d in range(5):
            target = w.seq * BLK + b + d - 2
            chosen = (off_ref[b, 0] == d - 2) | (off_ref[b, 1] == d - 2) | (off_ref[b, 2] == d - 2)
            usable = chosen & (target >= 0) & (target < nblk)
            parts.append(scores[d * NB : (d + 1) * NB] + jnp.where(usable, 0.0, -1e30))
        scores = jnp.concatenate(parts + [scores[NEAR:]], 0)
        peak = jnp.max(scores, 0, keepdims=True)
        exps = jnp.exp(scores - peak)
        prob = exps * (1.0 / jnp.sum(exps, 0, keepdims=True))
        prob_b = prob.astype(BF16)
        probs[b] = prob
        halves[b] = prob_b
        att[b * NB : (b + 1) * NB] = collect(dot_tn(prob_b, vals)).astype(BF16)

    for t in range(tps):
        part = dot_tn(att[...], ogs[t]).astype(BF16)
        for j in range(COLS // LANE):
            for i in range(TOK // SUB):
                wpart[spots[(t * 2 + j) * 16 + i]] = part[i * SUB : (i + 1) * SUB, j * LANE : (j + 1) * LANE]
    weight = Scatter(flights, w, wpart, wgot1, wrows, wgot2, s_w1, r_w1, s_w2, r_w2, 5 if n == 8 else n - 1)
    whole = Gather(flights, w, wfull, s_w3, r_w3, s_w4, r_w4)
    weight.begin()

    for t in range(tps):
        msend[t] = dot_nn(att[...], w_ref[:, t * COLS : (t + 1) * COLS]).astype(BF16)

    def move_mix(act):
        def one(k):
            c, device = w.tp_at(k)
            act(remote(msend.at[c], mgot.at[k], s_m.at[k], r_m.at[k], device))

        each(1, tps, one)

    mix = Flight(flights, move_mix)
    mix.begin()
    mine_out[...] = dot_nn(att[...], w_ref[:, pl.ds(pl.multiple_of(w.tp * COLS, COLS), COLS)])

    for b in range(BLK):
        keys = listed_rows(kpad, kft, b)
        vals = listed_rows(vpad, vft, b)
        q_diag = diagonal(q_ref[b * NB : (b + 1) * NB])
        g_diag = diagonal(gatt[b * NB : (b + 1) * NB])
        prob = probs[b]
        dprob = dot_nt(vals, g_diag)
        inner = jnp.sum(prob * dprob, 0, keepdims=True)
        dscore = (prob * (dprob - inner) * 0.125).astype(BF16)
        gq_ref[b * NB : (b + 1) * NB] = collect(dot_tn(dscore, keys)).astype(BF16)
        dkey = dot_nn(dscore, q_diag)
        dval = dot_nn(halves[b], g_diag)
        gkpad[b * NB : b * NB + NEAR] += dkey[:NEAR]
        gvpad[b * NB : b * NB + NEAR] += dval[:NEAR]
        for r in range(BLK):
            for c in range(4):
                s = c * BLK + r
                src = dkey if c < 2 else dval
                dlist[b * C1 : (b + 1) * C1, s * LANE : (s + 1) * LANE] = src[
                    NEAR + r * C1 : NEAR + (r + 1) * C1, (c % 2) * LANE : (c % 2 + 1) * LANE
                ].astype(BF16)
        dtop[:, :COLS] += dkey[NEAR + FAR :]
        dtop[:, COLS:] += dval[NEAR + FAR :]

    for i, pad in enumerate((gkpad, gvpad)):
        hsend[i] = pad[half + TOK :].astype(BF16)
        hsend[2 + i] = pad[:half].astype(BF16)

    def move_back(act):
        for i in range(2):
            act(remote(hsend.at[i], hgot.at[i], s_b.at[i], r_b.at[i], w.step(1)))
            act(remote(hsend.at[2 + i], hgot.at[2 + i], s_b.at[2 + i], r_b.at[2 + i], w.step(-1)))

    tile_grad = dot_tn(hot[...], dlist[...])
    cols = []
    for c in range(4):
        for r in range(BLK):
            s = c * BLK + r
            cols.append(tile_grad[:, s * LANE : (s + 1) * LANE] + dtop[:, c * LANE : (c + 1) * LANE] * 0.5)
    by_row = jnp.concatenate(
        [
            jnp.concatenate([cols[s][g * group : (g + 1) * group] for s in range(SUB)], 0)
            for g in range(groups)
        ],
        1,
    ).astype(BF16)
    packed = dot_nn(swap_back, by_row).astype(BF16)
    for g in range(groups):
        fpart[g * group : (g + 1) * group] = packed[:, g * LANE : (g + 1) * LANE].reshape(group, SUB, LANE)
    halo_back = Flight(flights, move_back)
    halo_back.begin()
    coupled = Scatter(flights, w, fpart, fgot1, frows, fgot2, s_f1, r_f1, s_f2, r_f2, 0)
    coupled.begin()

    weight.forward()

    mix.land()
    total = mine_out[...]
    for k in range(1, tps):
        total += mgot[k].astype(F32)
    mixed_ref[...] = total.astype(BF16)
    taken = [
        pltpu.make_async_copy(src, dst, s_out.at[i])
        for i, (src, dst) in enumerate(
            ((mixed_ref, mixed_out), (gq_ref, gq_out), (gk_ref, gk_out), (gv_ref, gv_out), (wfull, pieces_out))
        )
    ]
    for copy in taken[:2]:
        copy.start()
    halo_back.land()

    wfull[w.xh * n * n] = weight.land().astype(BF16)
    whole.begin()
    coupled.forward()
    whole.forward()

    fine_grad = coupled.land() * 0.125
    for i, (pad, out) in enumerate(((gkpad, gk_ref), (gvpad, gv_ref))):
        for r in range(BLK):
            rows = pad[half + r * NB : half + (r + 1) * NB]
            if r < BLK // 2:
                rows += hgot[i, r * NB : (r + 1) * NB].astype(F32)
            else:
                rows += hgot[2 + i, r * NB - half : (r + 1) * NB - half].astype(F32)
            for c in range(2):
                s = (2 * i + c) * BLK + r
                out[r * NB : (r + 1) * NB, c * LANE : (c + 1) * LANE] = (
                    rows[:, c * LANE : (c + 1) * LANE] + fine_grad[s : s + 1]
                ).astype(BF16)
    for copy in taken[2:4]:
        copy.start()

    whole.land()
    taken[4].start()
    for flight in flights:
        flight.end()
    for copy in taken:
        copy.wait()


def hand_over(n, tps, *refs):
    given, made, held, pieces, weight, sems_in, sems_out = refs[:5], refs[5:10], refs[10:14], *refs[14:]
    into = [pltpu.make_async_copy(src, dst, sems_in.at[i]) for i, (src, dst) in enumerate(zip(given, (*held, pieces)))]
    for i in (4, 0, 1, 2, 3):
        into[i].start()
    out = [pltpu.make_async_copy(src, dst, sems_out.at[i]) for i, (src, dst) in enumerate(zip(held, made))]
    spots = Place(n, tps).spots()
    into[4].wait()
    for j in range(tps * COLS // LANE):
        cols = pl.ds(j * LANE, LANE)
        for i in range(TOK // SUB):
            weight[i * SUB : (i + 1) * SUB, cols] = pieces[spots[j * 16 + i]].astype(F32)
        out.append(pltpu.make_async_copy(weight.at[:, cols], made[4].at[:, cols], sems_out.at[4 + j]))
        out[-1].start()
        if j < 4:
            into[j].wait()
            out[j].start()
    for j in range(tps * COLS // LANE, 4):
        into[j].wait()
        out[j].start()
    for copy in out:
        copy.wait()


def shards(n, tps, queries, keys, values, out_weight, out_grad, near_offsets, coupling):
    tiles = 2 * n * n
    group = min(16, tiles)
    pieces = (tiles, SUB, LANE)
    dma = lambda *shape: pltpu.SemaphoreType.DMA(shape)
    vm = lambda dtype, *shape: pltpu.VMEM(shape, dtype)
    pair = [dma(2, n)] * 2
    relays = [dma(8, n)] * 2
    rowwise = [dma(2, 2, n)] * 2
    keep = [vm(BF16, TOK, COLS)] * 4
    in_place = pl.BlockSpec(memory_space=pltpu.HBM)
    rest = FAR + tiles
    length = NEAR + rest
    sums = [vm(BF16, *pieces), vm(BF16, 2, n, n, SUB, LANE), vm(BF16, 2, n, SUB, LANE), vm(BF16, 2, n, SUB, LANE)]
    scratch = [
        pltpu.SMEM(near_offsets.shape, jnp.int32), pltpu.SMEM(coupling.shape, jnp.int32),
        *(vm(BF16, *x.shape) for x in (queries, keys, values, out_weight, out_grad)), dma(7),
        *keep, dma(5),
        vm(BF16, 2 * TOK, COLS), vm(BF16, 2 * TOK, COLS), vm(BF16, *pieces), vm(BF16, tps, TOK, COLS),
        vm(BF16, BLK, rest, COLS), vm(BF16, BLK, rest, COLS), vm(BF16, BLK * C1, tiles),
        vm(F32, BLK, length, COLS), vm(BF16, BLK, length, COLS), vm(BF16, TOK, COLS), vm(BF16, TOK, COLS), vm(F32, TOK, COLS),
        vm(BF16, tps, TOK, COLS), vm(BF16, tps, TOK, COLS), vm(F32, 2 * TOK, COLS), vm(F32, 2 * TOK, COLS),
        vm(BF16, 4, TOK // 2, COLS), vm(BF16, 4, TOK // 2, COLS), vm(BF16, BLK * C1, SUB * LANE), vm(F32, tiles, 2 * COLS),
        *sums, vm(BF16, *pieces), *sums,
        dma(4), dma(4), dma(tps), dma(tps), dma(tps), dma(tps), dma(4), dma(4),
        *pair, *relays, *rowwise, *pair, *pair, *relays, *rowwise, *pair,
    ]
    like = lambda x: jax.ShapeDtypeStruct(x.shape, BF16)
    shapes = (like(out_grad), like(queries), like(keys), like(values))
    weight_grad = jax.ShapeDtypeStruct(out_weight.shape, F32)
    results = pl.pallas_call(
        functools.partial(kernel, n, tps, group),
        out_shape=(*shapes, jax.ShapeDtypeStruct(pieces, BF16)),
        in_specs=[in_place] * 7,
        out_specs=[in_place] * 5,
        scratch_shapes=scratch,
        compiler_params=pltpu.CompilerParams(collective_id=0, has_side_effects=True, vmem_limit_bytes=VMEM),
    )(near_offsets, coupling, queries, keys, values, out_weight, out_grad)
    return pl.pallas_call(
        functools.partial(hand_over, n, tps),
        out_shape=(*shapes, weight_grad),
        in_specs=[in_place] * 5,
        out_specs=[in_place] * 5,
        scratch_shapes=[*keep, vm(BF16, *pieces), vm(F32, *out_weight.shape), dma(5), dma(4 + tps * COLS // LANE)],
        compiler_params=pltpu.CompilerParams(vmem_limit_bytes=VMEM),
    )(*results)


def solution(mesh):
    n = int(round((mesh.shape["seq"] // 2) ** 0.5))
    step = functools.partial(shards, n, mesh.shape["tp"])
    in_specs = (
        P("seq", "tp"),
        P("seq", "tp"),
        P("seq", "tp"),
        P("tp", None),
        P("seq", "tp"),
        P("seq", None),
        P("seq", None),
    )
    out_specs = (P("seq", "tp"), P("seq", "tp"), P("seq", "tp"), P("seq", "tp"), P("tp", None))
    return jax.shard_map(step, mesh=mesh, in_specs=in_specs, out_specs=out_specs, check_vma=False)
```

```python
import functools

import jax
import jax.numpy as jnp
from jax import lax
from jax.experimental import pallas as pl
from jax.experimental.pallas import tpu as pltpu
from jax.sharding import PartitionSpec as P

MESH = pl.DeviceIdType.MESH
F32 = jnp.float32
BF16 = jnp.bfloat16
HD = 64
NB = 64
BLK = 4
HEADS = 4
COLS = HEADS * HD
TOK = BLK * NB
C1 = 16
LANE = 128
SUB = 16
NEAR = 5 * NB
FAR = C1 * BLK
VMEM = 48 * 1024 * 1024


def each(low, high, body):
    lax.fori_loop(low, high, lambda k, c: (body(low + high - 1 - k), c)[1], 0)


def dot_nn(a, b):
    return lax.dot_general(a, b, (((1,), (0,)), ((), ())), preferred_element_type=F32)


def dot_nt(a, b):
    return lax.dot_general(a, b, (((1,), (1,)), ((), ())), preferred_element_type=F32)


def dot_tn(a, b):
    return lax.dot_general(a, b, (((0,), (0,)), ((), ())), preferred_element_type=F32)


def iota(shape, dim):
    return lax.broadcasted_iota(jnp.int32, shape, dim)


class Place:
    def __init__(self, n, tps):
        self.n, self.tps = n, tps
        self.seqs = 2 * n * n
        self.seq = lax.axis_index("seq")
        self.tp = lax.axis_index("tp")
        self.z = lax.div(self.seq, 2 * n)
        self.y = lax.rem(lax.div(self.seq, 2), n)
        self.xh = lax.rem(self.seq, 2)
        self.mine = self.z * (1 - self.xh) + self.y * self.xh
        self.cross = self.y * (1 - self.xh) + self.z * self.xh

    def by(self, slot):
        odd = lax.rem(slot, 2)
        return odd * lax.div(slot + 1, 2) + (1 - odd) * (self.n - lax.div(slot, 2))

    def back(self, slot):
        return slot + 2 * lax.rem(slot, 2) - 1 - lax.div(slot, self.n - 1)

    def slot(self, ahead):
        n = self.n
        upper = lax.div(n - 1 + n // 2 - ahead, n - 1)
        return upper * (2 * ahead - 1) + (1 - upper) * 2 * (n - ahead) + lax.div(n - 1 - ahead, n - 1)

    def at(self, z, y, xh):
        return (z * (2 * self.n) + y * 2 + xh, self.tp)

    def along_mine(self, slot, xh):
        c = lax.rem(self.mine + self.by(slot), self.n)
        return self.at(c * (1 - self.xh) + self.z * self.xh, self.y * (1 - self.xh) + c * self.xh, xh)

    def along_cross(self, slot, xh):
        c = lax.rem(self.cross + self.by(slot), self.n)
        return self.at(self.z * (1 - self.xh) + c * self.xh, c * (1 - self.xh) + self.y * self.xh, xh)

    def along_y(self, slot):
        return self.at(self.z, lax.rem(self.y + self.by(slot), self.n), self.xh)

    def along_z(self, slot):
        return self.at(lax.rem(self.z + self.by(slot), self.n), self.y, self.xh)

    def step(self, by):
        return (lax.rem(self.seq + self.seqs + by, self.seqs), self.tp)

    def tp_at(self, k):
        c = lax.rem(self.tp + k, self.tps)
        return c, (self.seq, c)

    def spots(self):
        n = self.n
        of_y = [self.slot(lax.rem(c + n - self.y, n)) for c in range(n)]
        of_z = [self.slot(lax.rem(c + n - self.z, n)) for c in range(n)]
        return [
            h * n * n + (of_z if h else of_y)[r] * n + (of_y if h else of_z)[c]
            for h in range(2)
            for r in range(n)
            for c in range(n)
        ]


def remote(src, dst, send, recv, device):
    return pltpu.make_async_remote_copy(
        src_ref=src, dst_ref=dst, send_sem=send, recv_sem=recv, device_id=device, device_id_type=MESH
    )


class Flight:
    def __init__(self, log, move, *args):
        self.move, self.args = move, args
        log.append(self)

    def begin(self):
        self.move(*self.args, lambda copy: copy.start())

    def land(self):
        self.move(*self.args, lambda copy: copy.wait_recv())

    def end(self):
        self.move(*self.args, lambda copy: copy.wait_send())


def spread(w, buf, send, recv, other, low, high, act):
    own = buf.at[w.xh * w.n * w.n]

    def one(i):
        into = buf.at[w.xh * w.n * w.n + w.back(i)]
        xh = 1 - w.xh if other else w.xh
        act(remote(own, into, send.at[other, i], recv.at[other, w.back(i)], w.along_mine(i, xh)))

    if low == 0:
        if other:
            act(remote(own, own, send.at[1, 0], recv.at[1, 0], w.at(w.z, w.y, 1 - w.xh)))
        low = 1
    each(low, high, one)


def relay(w, buf, send, recv, batch, other, low, high, act):
    n = w.n
    base = (1 - w.xh if other else w.xh) * n * n

    def one(i):
        j = w.back(i)
        mine = buf.at[pl.ds(base + low, high - low)]
        into = buf.at[pl.ds(base + j * n + low, high - low)]
        device = (w.along_mine if other else w.along_cross)(i, w.xh)
        act(remote(mine, into, send.at[batch, i], recv.at[batch, j], device))

    each(1, n, one)


class Gather:
    def __init__(self, log, w, buf, s_1, r_1, s_2, r_2):
        n = w.n
        cuts = [c for c in (1, 3, 5, 8) if c < n] + [n]
        same = list(zip([0] + cuts[:-1], cuts))
        cross = [(0, cuts[1])] + same[2:]
        self.out = [Flight(log, spread, w, buf, s_1, r_1, 1, 0, n), Flight(log, spread, w, buf, s_1, r_1, 0, 0, n)]
        steps = [(0, *part) for part in same] + [(1, *part) for part in cross]
        steps.sort(key=lambda step: (step[1] + 2 * step[0], step[0]))
        self.arrive = [Flight([], spread, w, buf, s_1, r_1, *step) for step in steps]
        self.onward = [Flight(log, relay, w, buf, s_2, r_2, i, *step) for i, step in enumerate(steps)]

    def begin(self):
        self.out[1].begin()
        self.out[0].begin()
        self.onward[0].begin()

    def forward(self):
        for arrived, onward in zip(self.arrive[1:], self.onward[1:]):
            arrived.land()
            onward.begin()

    def land(self):
        for onward in self.onward:
            onward.land()


def to_rows(w, part, got, send, recv, batch, low, high, act):
    n = w.n

    def one(i):
        for h, device in ((0, w.along_y(i)), (1, w.along_z(i))):
            mine = part.at[pl.ds(h * n * n + i * n + low, high - low)]
            act(remote(mine, got.at[h, i, pl.ds(low, high - low)], send.at[batch, h, i], recv.at[batch, h, i], device))

    each(1, n, one)


def to_owners(w, rows, got, send, recv, low, high, act):
    def same(i):
        act(remote(rows.at[w.xh, i], got.at[0, i], send.at[0, i], recv.at[0, i], w.along_mine(i, w.xh)))

    def other(i):
        act(remote(rows.at[1 - w.xh, i], got.at[1, i], send.at[1, i], recv.at[1, i], w.along_cross(i, 1 - w.xh)))

    each(max(low, 1), high, same)
    if low == 0:
        act(remote(rows.at[1 - w.xh, 0], got.at[1, 0], send.at[1, 0], recv.at[1, 0], w.at(w.z, w.y, 1 - w.xh)))
    each(max(low, 1), high, other)


class Scatter:
    def __init__(self, log, w, part, got_1, rows, got_2, s_1, r_1, s_2, r_2, cut):
        n = w.n
        self.w, self.part, self.got_1, self.rows, self.got_2 = w, part, got_1, rows, got_2
        self.cols = [(cut, n), (0, cut)] if cut else [(0, n)]
        self.first = [Flight(log, to_rows, w, part, got_1, s_1, r_1, i, *c) for i, c in enumerate(self.cols)]
        self.second = [Flight(log, to_owners, w, rows, got_2, s_2, r_2, *c) for c in self.cols]

    def begin(self):
        for first in self.first:
            first.begin()

    def forward(self):
        n = self.w.n
        for (low, high), first, second in zip(self.cols, self.first, self.second):
            first.land()
            for h in range(2):
                total = self.part[h * n * n + low : h * n * n + high].astype(F32)
                for i in range(1, n):
                    total += self.got_1[h, i, low:high].astype(F32)
                self.rows[h, low:high] = total.astype(BF16)
            second.begin()

    def land(self):
        for second in self.second:
            second.land()
        total = self.rows[self.w.xh, 0].astype(F32)
        for i in range(1, self.w.n):
            total += self.got_2[0, i].astype(F32)
        for i in range(self.w.n):
            total += self.got_2[1, i].astype(F32)
        return total


def kernel(
    n, tps, group,
    off_in, cpl_in, q_in, k_in, v_in, w_in, og_in,
    mixed_ref, gq_ref, gk_ref, gv_ref, pieces_ref,
    off_ref, cpl_ref, q_ref, k_ref, v_ref, w_ref, og_ref, s_in,
    kpad, vpad, fine, ogs, kft, vft, hot, probs, halves, att, gatt, mine_out,
    msend, mgot, gkpad, gvpad, hsend, hgot, dlist, dtop,
    wpart, wgot1, wrows, wgot2, wfull, fpart, fgot1, frows, fgot2,
    s_h, r_h, s_o, r_o, s_m, r_m, s_b, r_b,
    s_g1, r_g1, s_g2, r_g2, s_w1, r_w1, s_w2, r_w2, s_w3, r_w3, s_w4, r_w4, s_f1, r_f1, s_f2, r_f2,
):
    w = Place(n, tps)
    tiles = w.seqs
    groups = tiles // group
    nblk = tiles * BLK
    half = TOK // 2
    flights = []

    brought = [
        pltpu.make_async_copy(src, dst, s_in.at[i])
        for i, (src, dst) in enumerate(
            ((k_in, k_ref), (v_in, v_ref), (og_in, og_ref), (cpl_in, cpl_ref), (off_in, off_ref), (q_in, q_ref), (w_in, w_ref))
        )
    ]
    for copy in brought:
        copy.start()

    barrier = pltpu.get_barrier_semaphore()

    def greet(device):
        pl.semaphore_signal(barrier, inc=1, device_id=device, device_id_type=MESH)

    def greet_square(i):
        greet(w.along_y(i))
        greet(w.along_z(i))
        greet(w.along_mine(i, 1 - w.xh))
        greet(w.along_cross(i, 1 - w.xh))

    each(1, n, greet_square)
    greet(w.at(w.z, w.y, 1 - w.xh))
    greet(w.step(1))
    greet(w.step(-1))
    each(1, tps, lambda k: greet(w.tp_at(k)[1]))

    for copy in brought[:2]:
        copy.wait()
    piece = jnp.zeros((SUB, LANE), F32)
    for c in range(4):
        row, tok = iota((SUB, TOK), 0), iota((SUB, TOK), 1)
        pick = jnp.where((row - c * BLK) == (tok >> 6), 1.0, 0.0).astype(BF16)
        src = k_ref if c < 2 else v_ref
        piece += dot_nn(pick, src[:, (c % 2) * LANE : (c % 2 + 1) * LANE])
    fine[w.xh * n * n] = (piece * 0.125).astype(BF16)
    pl.semaphore_wait(barrier, 4 * (n - 1) + 3 + tps - 1)

    def move_halo(act):
        for i, (src, pad) in enumerate(((k_ref, kpad), (v_ref, vpad))):
            act(remote(src.at[pl.ds(half, half)], pad.at[pl.ds(0, half)], s_h.at[i], r_h.at[i], w.step(1)))
            act(remote(src.at[pl.ds(0, half)], pad.at[pl.ds(half + TOK, half)], s_h.at[2 + i], r_h.at[2 + i], w.step(-1)))

    def move_columns(act):
        def one(k):
            act(remote(og_ref, ogs.at[w.tp], s_o.at[k], r_o.at[k], w.tp_at(k)[1]))

        each(1, tps, one)

    summaries = Gather(flights, w, fine, s_g1, r_g1, s_g2, r_g2)
    halo = Flight(flights, move_halo)
    columns = Flight(flights, move_columns)
    summaries.begin()
    halo.begin()
    brought[2].wait()
    columns.begin()

    ogs[w.tp] = og_ref[...]
    kpad[half : half + TOK] = k_ref[...]
    vpad[half : half + TOK] = v_ref[...]
    gkpad[...] = jnp.zeros_like(gkpad)
    gvpad[...] = jnp.zeros_like(gvpad)
    dtop[...] = jnp.zeros_like(dtop)
    for copy in brought[3:]:
        copy.wait()

    bits = n.bit_length() - 1
    place = iota((1, tiles), 1)

    def ahead(slot):
        return jnp.where((slot & 1) == 1, (slot + 1) >> 1, n - (slot >> 1))

    by_row, by_col = ahead((place >> bits) & (n - 1)), ahead(place & (n - 1))
    tile_of = jnp.where(
        place < n * n,
        ((w.z + by_col) & (n - 1)) * (2 * n) + ((w.y + by_row) & (n - 1)) * 2,
        ((w.z + by_row) & (n - 1)) * (2 * n) + ((w.y + by_col) & (n - 1)) * 2 + 1,
    )
    rows8 = iota((8, tiles), 0)
    listed = []
    for g in range(BLK * C1 // 8):
        wanted = jnp.zeros((8, tiles), jnp.int32)
        for i in range(8):
            at = g * 8 + i
            wanted = jnp.where(rows8 == i, cpl_ref[at // C1, at % C1], wanted)
        listed.append(wanted)
    wanted = jnp.concatenate(listed, 0)
    hot[...] = jnp.where(wanted == tile_of, 1.0, 0.0).astype(BF16)

    size = group * SUB
    to, fro = iota((size, size), 0), iota((size, size), 1)
    gbits = group.bit_length() - 1
    swapped = (fro & (SUB - 1)) * group + (fro >> 4)
    swap = jnp.where(to == swapped, 1.0, 0.0).astype(BF16)
    swapped = (fro & (group - 1)) * SUB + (fro >> gbits)
    swap_back = jnp.where(to == swapped, 1.0, 0.0).astype(BF16)

    head_of = iota((1, COLS), 1) >> 6
    masks = [jnp.where(head_of == h, 1.0, 0.0) for h in range(HEADS)]
    masks_b = [m.astype(BF16) for m in masks]

    def diagonal(rows):
        return jnp.concatenate([rows * m for m in masks_b], 0)

    def collect(full):
        out = full[0:NB] * masks[0]
        for h in range(1, HEADS):
            out += full[h * NB : (h + 1) * NB] * masks[h]
        return out

    summaries.forward()

    spots = w.spots()
    halo.land()
    summaries.land()

    packed = jnp.concatenate([fine[g * group : (g + 1) * group].reshape(size, LANE) for g in range(groups)], 1)
    by_row = dot_nn(swap, packed)
    flat = jnp.concatenate(
        [
            jnp.concatenate([by_row[s * group : (s + 1) * group, g * LANE : (g + 1) * LANE] for s in range(SUB)], 1)
            for g in range(groups)
        ],
        0,
    )
    tops = []
    for c in range(4):
        total = flat[:, c * BLK * LANE : (c * BLK + 1) * LANE]
        for r in range(1, BLK):
            total += flat[:, (c * BLK + r) * LANE : (c * BLK + r + 1) * LANE]
        tops.append((total * 0.5).astype(BF16))
    far = dot_nn(hot[...], flat.astype(BF16)).astype(BF16)
    for b in range(BLK):
        for r in range(BLK):
            for c in range(4):
                s = c * BLK + r
                into = kft if c < 2 else vft
                into[b, r * C1 : (r + 1) * C1, (c % 2) * LANE : (c % 2 + 1) * LANE] = far[
                    b * C1 : (b + 1) * C1, s * LANE : (s + 1) * LANE
                ]
        kft[b, FAR:, :LANE], kft[b, FAR:, LANE:] = tops[0], tops[1]
        vft[b, FAR:, :LANE], vft[b, FAR:, LANE:] = tops[2], tops[3]

    def listed_rows(pad, rest, b):
        return jnp.concatenate([pad[b * NB : b * NB + NEAR], rest[b]], 0)

    for b in range(BLK):
        keys = listed_rows(kpad, kft, b)
        vals = listed_rows(vpad, vft, b)
        scores = dot_nt(keys, diagonal(q_ref[b * NB : (b + 1) * NB])) * 0.125
        parts = []
        for d in range(5):
            target = w.seq * BLK + b + d - 2
            chosen = (off_ref[b, 0] == d - 2) | (off_ref[b, 1] == d - 2) | (off_ref[b, 2] == d - 2)
            usable = chosen & (target >= 0) & (target < nblk)
            parts.append(scores[d * NB : (d + 1) * NB] + jnp.where(usable, 0.0, -1e30))
        scores = jnp.concatenate(parts + [scores[NEAR:]], 0)
        peak = jnp.max(scores, 0, keepdims=True)
        exps = jnp.exp(scores - peak)
        prob = exps * (1.0 / jnp.sum(exps, 0, keepdims=True))
        prob_b = prob.astype(BF16)
        probs[b] = prob
        halves[b] = prob_b
        att[b * NB : (b + 1) * NB] = collect(dot_tn(prob_b, vals)).astype(BF16)

    columns.land()
    for t in range(tps):
        part = dot_tn(att[...], ogs[t]).astype(BF16)
        for j in range(COLS // LANE):
            for i in range(TOK // SUB):
                wpart[spots[(t * 2 + j) * 16 + i]] = part[i * SUB : (i + 1) * SUB, j * LANE : (j + 1) * LANE]
    weight = Scatter(flights, w, wpart, wgot1, wrows, wgot2, s_w1, r_w1, s_w2, r_w2, 5 if n == 8 else n - 1)
    whole = Gather(flights, w, wfull, s_w3, r_w3, s_w4, r_w4)
    weight.begin()

    for t in range(tps):
        msend[t] = dot_nn(att[...], w_ref[:, t * COLS : (t + 1) * COLS]).astype(BF16)

    def move_mix(act):
        def one(k):
            c, device = w.tp_at(k)
            act(remote(msend.at[c], mgot.at[k], s_m.at[k], r_m.at[k], device))

        each(1, tps, one)

    mix = Flight(flights, move_mix)
    mix.begin()
    mine_out[...] = dot_nn(att[...], w_ref[:, pl.ds(pl.multiple_of(w.tp * COLS, COLS), COLS)])

    grad = dot_nt(ogs[0], w_ref[:, 0:COLS])
    for t in range(1, tps):
        grad += dot_nt(ogs[t], w_ref[:, t * COLS : (t + 1) * COLS])
    gatt[...] = grad.astype(BF16)

    for b in range(BLK):
        keys = listed_rows(kpad, kft, b)
        vals = listed_rows(vpad, vft, b)
        q_diag = diagonal(q_ref[b * NB : (b + 1) * NB])
        g_diag = diagonal(gatt[b * NB : (b + 1) * NB])
        prob = probs[b]
        dprob = dot_nt(vals, g_diag)
        inner = jnp.sum(prob * dprob, 0, keepdims=True)
        dscore = (prob * (dprob - inner) * 0.125).astype(BF16)
        gq_ref[b * NB : (b + 1) * NB] = collect(dot_tn(dscore, keys)).astype(BF16)
        dkey = dot_nn(dscore, q_diag)
        dval = dot_nn(halves[b], g_diag)
        gkpad[b * NB : b * NB + NEAR] += dkey[:NEAR]
        gvpad[b * NB : b * NB + NEAR] += dval[:NEAR]
        for r in range(BLK):
            for c in range(4):
                s = c * BLK + r
                src = dkey if c < 2 else dval
                dlist[b * C1 : (b + 1) * C1, s * LANE : (s + 1) * LANE] = src[
                    NEAR + r * C1 : NEAR + (r + 1) * C1, (c % 2) * LANE : (c % 2 + 1) * LANE
                ].astype(BF16)
        dtop[:, :COLS] += dkey[NEAR + FAR :]
        dtop[:, COLS:] += dval[NEAR + FAR :]

    for i, pad in enumerate((gkpad, gvpad)):
        hsend[i] = pad[half + TOK :].astype(BF16)
        hsend[2 + i] = pad[:half].astype(BF16)

    def move_back(act):
        for i in range(2):
            act(remote(hsend.at[i], hgot.at[i], s_b.at[i], r_b.at[i], w.step(1)))
            act(remote(hsend.at[2 + i], hgot.at[2 + i], s_b.at[2 + i], r_b.at[2 + i], w.step(-1)))

    tile_grad = dot_tn(hot[...], dlist[...])
    cols = []
    for c in range(4):
        for r in range(BLK):
            s = c * BLK + r
            cols.append(tile_grad[:, s * LANE : (s + 1) * LANE] + dtop[:, c * LANE : (c + 1) * LANE] * 0.5)
    by_row = jnp.concatenate(
        [
            jnp.concatenate([cols[s][g * group : (g + 1) * group] for s in range(SUB)], 0)
            for g in range(groups)
        ],
        1,
    ).astype(BF16)
    packed = dot_nn(swap_back, by_row).astype(BF16)
    for g in range(groups):
        fpart[g * group : (g + 1) * group] = packed[:, g * LANE : (g + 1) * LANE].reshape(group, SUB, LANE)
    halo_back = Flight(flights, move_back)
    halo_back.begin()
    coupled = Scatter(flights, w, fpart, fgot1, frows, fgot2, s_f1, r_f1, s_f2, r_f2, 0)

    weight.forward()
    coupled.begin()

    mix.land()
    total = mine_out[...]
    for k in range(1, tps):
        total += mgot[k].astype(F32)
    mixed_ref[...] = total.astype(BF16)
    halo_back.land()

    wfull[w.xh * n * n] = weight.land().astype(BF16)
    whole.begin()
    coupled.forward()
    whole.forward()

    fine_grad = coupled.land() * 0.125
    for i, (pad, out) in enumerate(((gkpad, gk_ref), (gvpad, gv_ref))):
        for r in range(BLK):
            rows = pad[half + r * NB : half + (r + 1) * NB]
            if r < BLK // 2:
                rows += hgot[i, r * NB : (r + 1) * NB].astype(F32)
            else:
                rows += hgot[2 + i, r * NB - half : (r + 1) * NB - half].astype(F32)
            for c in range(2):
                s = (2 * i + c) * BLK + r
                out[r * NB : (r + 1) * NB, c * LANE : (c + 1) * LANE] = (
                    rows[:, c * LANE : (c + 1) * LANE] + fine_grad[s : s + 1]
                ).astype(BF16)

    for flight in flights:
        if flight not in whole.onward:
            flight.end()
    whole.land()
    pieces_ref[...] = wfull[...]
    for onward in whole.onward:
        onward.end()


def hand_over(n, tps, *refs):
    held, pieces, made, weight, sems = refs[:4], refs[4], refs[5:10], *refs[10:]
    out = [pltpu.make_async_copy(src, dst, sems.at[i]) for i, (src, dst) in enumerate(zip(held, made))]
    for copy in out:
        copy.start()
    spots = Place(n, tps).spots()
    for j in range(tps * COLS // LANE):
        cols = pl.ds(j * LANE, LANE)
        for i in range(TOK // SUB):
            weight[i * SUB : (i + 1) * SUB, cols] = pieces[spots[j * 16 + i]].astype(F32)
        out.append(pltpu.make_async_copy(weight.at[:, cols], made[4].at[:, cols], sems.at[4 + j]))
        out[-1].start()
    for copy in out:
        copy.wait()


def shards(n, tps, queries, keys, values, out_weight, out_grad, near_offsets, coupling):
    tiles = 2 * n * n
    group = min(16, tiles)
    pieces = (tiles, SUB, LANE)
    dma = lambda *shape: pltpu.SemaphoreType.DMA(shape)
    vm = lambda dtype, *shape: pltpu.VMEM(shape, dtype)
    pair = [dma(2, n)] * 2
    relays = [dma(8, n)] * 2
    rowwise = [dma(2, 2, n)] * 2
    in_vmem = pl.BlockSpec(memory_space=pltpu.VMEM)
    in_place = pl.BlockSpec(memory_space=pltpu.HBM)
    rest = FAR + tiles
    length = NEAR + rest
    sums = [vm(BF16, *pieces), vm(BF16, 2, n, n, SUB, LANE), vm(BF16, 2, n, SUB, LANE), vm(BF16, 2, n, SUB, LANE)]
    scratch = [
        pltpu.SMEM(near_offsets.shape, jnp.int32), pltpu.SMEM(coupling.shape, jnp.int32),
        *(vm(BF16, *x.shape) for x in (queries, keys, values, out_weight, out_grad)), dma(7),
        vm(BF16, 2 * TOK, COLS), vm(BF16, 2 * TOK, COLS), vm(BF16, *pieces), vm(BF16, tps, TOK, COLS),
        vm(BF16, BLK, rest, COLS), vm(BF16, BLK, rest, COLS), vm(BF16, BLK * C1, tiles),
        vm(F32, BLK, length, COLS), vm(BF16, BLK, length, COLS), vm(BF16, TOK, COLS), vm(BF16, TOK, COLS), vm(F32, TOK, COLS),
        vm(BF16, tps, TOK, COLS), vm(BF16, tps, TOK, COLS), vm(F32, 2 * TOK, COLS), vm(F32, 2 * TOK, COLS),
        vm(BF16, 4, TOK // 2, COLS), vm(BF16, 4, TOK // 2, COLS), vm(BF16, BLK * C1, SUB * LANE), vm(F32, tiles, 2 * COLS),
        *sums, vm(BF16, *pieces), *sums,
        dma(4), dma(4), dma(tps), dma(tps), dma(tps), dma(tps), dma(4), dma(4),
        *pair, *relays, *rowwise, *pair, *pair, *relays, *rowwise, *pair,
    ]
    like = lambda x: jax.ShapeDtypeStruct(x.shape, BF16)
    shapes = (like(out_grad), like(queries), like(keys), like(values))
    weight_grad = jax.ShapeDtypeStruct(out_weight.shape, F32)
    results = pl.pallas_call(
        functools.partial(kernel, n, tps, group),
        out_shape=(*(pltpu.VMEM(x.shape, BF16) for x in shapes), pltpu.VMEM(pieces, BF16)),
        in_specs=[in_place] * 7,
        out_specs=[in_vmem] * 5,
        scratch_shapes=scratch,
        compiler_params=pltpu.CompilerParams(collective_id=0, has_side_effects=True, vmem_limit_bytes=VMEM),
    )(*(
        pltpu.with_memory_space_constraint(x, pltpu.HBM)
        for x in (near_offsets, coupling, queries, keys, values, out_weight, out_grad)
    ))
    return pl.pallas_call(
        functools.partial(hand_over, n, tps),
        out_shape=(*shapes, weight_grad),
        in_specs=[in_vmem] * 5,
        out_specs=[in_place] * 5,
        scratch_shapes=[vm(F32, *out_weight.shape), dma(4 + tps * COLS // LANE)],
        compiler_params=pltpu.CompilerParams(vmem_limit_bytes=VMEM),
    )(*results)


def solution(mesh):
    n = int(round((mesh.shape["seq"] // 2) ** 0.5))
    step = functools.partial(shards, n, mesh.shape["tp"])
    in_specs = (
        P("seq", "tp"),
        P("seq", "tp"),
        P("seq", "tp"),
        P("tp", None),
        P("seq", "tp"),
        P("seq", None),
        P("seq", None),
    )
    out_specs = (P("seq", "tp"), P("seq", "tp"), P("seq", "tp"), P("seq", "tp"), P("tp", None))
    return jax.shard_map(step, mesh=mesh, in_specs=in_specs, out_specs=out_specs, check_vma=False)
```

```python
import functools

import jax
import jax.numpy as jnp
from jax import lax
from jax.experimental import pallas as pl
from jax.experimental.pallas import tpu as pltpu
from jax.sharding import PartitionSpec as P

MESH = pl.DeviceIdType.MESH
F32 = jnp.float32
BF16 = jnp.bfloat16
HD = 64
NB = 64
BLK = 4
HEADS = 4
COLS = HEADS * HD
TOK = BLK * NB
C1 = 16
LANE = 128
SUB = 16
NEAR = 5 * NB
FAR = C1 * BLK
VMEM = 48 * 1024 * 1024
SENDS, RECVS = 28, 36


def each(low, high, body):
    for k in range(high - 1, low - 1, -1):
        body(k)


def dot_nn(a, b):
    return lax.dot_general(a, b, (((1,), (0,)), ((), ())), preferred_element_type=F32)


def dot_nt(a, b):
    return lax.dot_general(a, b, (((1,), (1,)), ((), ())), preferred_element_type=F32)


def dot_tn(a, b):
    return lax.dot_general(a, b, (((0,), (0,)), ((), ())), preferred_element_type=F32)


def iota(shape, dim):
    return lax.broadcasted_iota(jnp.int32, shape, dim)


class Place:
    def __init__(self, n, tps):
        self.n, self.tps = n, tps
        self.seqs = 2 * n * n
        self.seq = lax.axis_index("seq")
        self.tp = lax.axis_index("tp")
        self.z = lax.div(self.seq, 2 * n)
        self.y = lax.rem(lax.div(self.seq, 2), n)
        self.xh = lax.rem(self.seq, 2)
        self.mine = self.z * (1 - self.xh) + self.y * self.xh
        self.cross = self.y * (1 - self.xh) + self.z * self.xh

    def by(self, slot):
        return (slot + 1) // 2 if slot % 2 else self.n - slot // 2

    def back(self, slot):
        return slot if slot == self.n - 1 else slot + 1 if slot % 2 else slot - 1

    def slot(self, ahead):
        n = self.n
        upper = lax.div(n - 1 + n // 2 - ahead, n - 1)
        return upper * (2 * ahead - 1) + (1 - upper) * 2 * (n - ahead) + lax.div(n - 1 - ahead, n - 1)

    def at(self, z, y, xh):
        return (z * (2 * self.n) + y * 2 + xh, self.tp)

    def along_mine(self, slot, xh):
        c = lax.rem(self.mine + self.by(slot), self.n)
        return self.at(c * (1 - self.xh) + self.z * self.xh, self.y * (1 - self.xh) + c * self.xh, xh)

    def along_cross(self, slot, xh):
        c = lax.rem(self.cross + self.by(slot), self.n)
        return self.at(self.z * (1 - self.xh) + c * self.xh, c * (1 - self.xh) + self.y * self.xh, xh)

    def along_y(self, slot):
        return self.at(self.z, lax.rem(self.y + self.by(slot), self.n), self.xh)

    def along_z(self, slot):
        return self.at(lax.rem(self.z + self.by(slot), self.n), self.y, self.xh)

    def step(self, by):
        return (lax.rem(self.seq + self.seqs + by, self.seqs), self.tp)

    def tp_at(self, k):
        c = lax.rem(self.tp + k, self.tps)
        return c, (self.seq, c)

    def spots(self):
        n = self.n
        of_y = [self.slot(lax.rem(c + n - self.y, n)) for c in range(n)]
        of_z = [self.slot(lax.rem(c + n - self.z, n)) for c in range(n)]
        return [
            h * n * n + (of_z if h else of_y)[r] * n + (of_y if h else of_z)[c]
            for h in range(2)
            for r in range(n)
            for c in range(n)
        ]


def remote(src, dst, send, recv, device):
    return pltpu.make_async_remote_copy(
        src_ref=src, dst_ref=dst, send_sem=send, recv_sem=recv, device_id=device, device_id_type=MESH
    )


class Log:
    def __init__(self, w, sends, recvs):
        self.w, self.sends, self.recvs = w, sends, recvs
        self.flights, self.sent, self.received = [], 0, 0

    def send(self):
        self.sent += 1
        return self.sends.at[self.sent - 1]

    def recv(self):
        self.received += 1
        return self.recvs.at[self.received - 1]

    def wait(self, size, send, recv):
        return remote(size, size, send, recv, self.w.at(self.w.z, self.w.y, 1 - self.w.xh))


class Flight:
    def __init__(self, log, move, size, recv=None):
        self.log, self.move, self.size = log, move, size
        self.send, self.recv = log.send(), log.recv() if recv is None else recv
        log.flights.append(self)

    def begin(self):
        self.move(lambda src, dst, device: remote(src, dst, self.send, self.recv, device).start())

    def land(self):
        self.log.wait(self.size, self.send, self.recv).wait_recv()

    def end(self):
        self.log.wait(self.size, self.send, self.recv).wait_send()


class Spread:
    def __init__(self, log, w, buf, other, steps):
        self.log, self.w, self.buf, self.other = log, w, buf, other
        self.send = log.send()
        self.recvs = {step: log.recv() for step in steps}
        log.flights.append(self)

    def count(self, low, high):
        return high - max(low, 1) + (1 if self.other and low == 0 else 0)

    def begin(self):
        w = self.w
        own = self.buf.at[w.xh * w.n * w.n]
        xh = 1 - w.xh if self.other else w.xh
        for i in range(w.n - 1, -1 if self.other else 0, -1):
            j = w.back(i) if i else 0
            recv = next(sem for (low, high), sem in self.recvs.items() if low <= j < high)
            into = self.buf.at[w.xh * w.n * w.n + j]
            device = w.along_mine(i, xh) if i else w.at(w.z, w.y, xh)
            remote(own, into, self.send, recv, device).start()

    def land(self, low, high):
        size = self.buf.at[pl.ds(0, self.count(low, high))]
        self.log.wait(size, self.send, self.recvs[low, high]).wait_recv()

    def end(self):
        size = self.buf.at[pl.ds(0, self.count(0, self.w.n))]
        self.log.wait(size, self.send, next(iter(self.recvs.values()))).wait_send()


class Gather:
    def __init__(self, log, w, buf):
        n = w.n
        self.w, self.buf = w, buf
        cuts = [c for c in (1, 3, 5, 8) if c < n] + [n]
        same = list(zip([0] + cuts[:-1], cuts))
        cross = [(0, cuts[1])] + same[2:]
        self.out = [Spread(log, w, buf, 0, same[1:]), Spread(log, w, buf, 1, cross)]
        self.steps = [(0, *part) for part in same] + [(1, *part) for part in cross]
        self.steps.sort(key=lambda step: (step[1] + 2 * step[0], step[0]))
        self.onward = [self.relay(log, *step) for step in self.steps]

    def relay(self, log, other, low, high):
        w, n, buf = self.w, self.w.n, self.buf
        base = (1 - w.xh if other else w.xh) * n * n
        mine = buf.at[pl.ds(base + low, high - low)]

        def move(copy):
            for i in range(n - 1, 0, -1):
                into = buf.at[pl.ds(base + w.back(i) * n + low, high - low)]
                copy(mine, into, (w.along_mine if other else w.along_cross)(i, w.xh))

        return Flight(log, move, buf.at[pl.ds(0, (n - 1) * (high - low))])

    def begin(self):
        self.out[1].begin()
        self.out[0].begin()
        self.onward[0].begin()

    def forward(self):
        for (other, low, high), onward in zip(self.steps[1:], self.onward[1:]):
            self.out[other].land(low, high)
            onward.begin()

    def land(self):
        for onward in self.onward:
            onward.land()


class Scatter:
    def __init__(self, log, w, part, got_1, rows, got_2, cut):
        n = w.n
        self.w, self.part, self.got_1, self.rows, self.got_2 = w, part, got_1, rows, got_2
        self.cols = [(cut, n), (0, cut)] if cut else [(0, n)]
        self.first = [self.to_rows(log, *c) for c in self.cols]
        self.second = [self.to_owners(log, *c) for c in self.cols]

    def to_rows(self, log, low, high):
        w, n = self.w, self.w.n

        def move(copy):
            for i in range(n - 1, 0, -1):
                for h, device in ((0, w.along_y(i)), (1, w.along_z(i))):
                    mine = self.part.at[pl.ds(h * n * n + i * n + low, high - low)]
                    copy(mine, self.got_1.at[h, i, pl.ds(low, high - low)], device)

        return Flight(log, move, self.part.at[pl.ds(0, 2 * (n - 1) * (high - low))])

    def to_owners(self, log, low, high):
        w = self.w

        def move(copy):
            for i in range(high - 1, max(low, 1) - 1, -1):
                copy(self.rows.at[1 - w.xh, i], self.got_2.at[1, i], w.along_cross(i, 1 - w.xh))
            if low == 0:
                copy(self.rows.at[1 - w.xh, 0], self.got_2.at[1, 0], w.at(w.z, w.y, 1 - w.xh))
            for i in range(high - 1, max(low, 1) - 1, -1):
                copy(self.rows.at[w.xh, i], self.got_2.at[0, i], w.along_mine(i, w.xh))

        count = 2 * (high - max(low, 1)) + (1 if low == 0 else 0)
        return Flight(log, move, self.part.at[pl.ds(0, count)])

    def begin(self):
        for first in self.first:
            first.begin()

    def forward(self):
        n = self.w.n
        for (low, high), first, second in zip(self.cols, self.first, self.second):
            first.land()
            for h in range(2):
                total = self.part[h * n * n + low : h * n * n + high].astype(F32)
                for i in range(1, n):
                    total += self.got_1[h, i, low:high].astype(F32)
                self.rows[h, low:high] = total.astype(BF16)
            second.begin()

    def land(self):
        for second in self.second:
            second.land()
        total = self.rows[self.w.xh, 0].astype(F32)
        for i in range(1, self.w.n):
            total += self.got_2[0, i].astype(F32)
        for i in range(self.w.n):
            total += self.got_2[1, i].astype(F32)
        return total


def kernel(
    n, tps, group,
    off_in, cpl_in, q_in, k_in, v_in, w_in, og_in,
    mixed_ref, gq_ref, gk_ref, gv_ref, pieces_ref,
    off_ref, cpl_ref, q_ref, k_ref, v_ref, w_ref, og_ref, s_in,
    kpad, vpad, fine, ogs, kft, vft, hot, probs, halves, att, gatt, mine_out,
    msend, mgot, gkpad, gvpad, hsend, hgot, dlist, dtop,
    wpart, wgot1, wrows, wgot2, wfull, fpart, fgot1, frows, fgot2,
    sends, recvs,
):
    w = Place(n, tps)
    tiles = w.seqs
    groups = tiles // group
    nblk = tiles * BLK
    half = TOK // 2
    log = Log(w, sends, recvs)

    barrier = pltpu.get_barrier_semaphore()

    def greet(device):
        pl.semaphore_signal(barrier, inc=1, device_id=device, device_id_type=MESH)

    def greet_square(i):
        greet(w.along_y(i))
        greet(w.along_z(i))
        greet(w.along_mine(i, 1 - w.xh))
        greet(w.along_cross(i, 1 - w.xh))

    each(1, n, greet_square)
    greet(w.at(w.z, w.y, 1 - w.xh))
    greet(w.step(1))
    greet(w.step(-1))
    each(1, tps, lambda k: greet(w.tp_at(k)[1]))

    brought = [
        pltpu.make_async_copy(src, dst, s_in.at[i])
        for i, (src, dst) in enumerate(
            ((k_in, k_ref), (v_in, v_ref), (og_in, og_ref), (cpl_in, cpl_ref), (off_in, off_ref), (q_in, q_ref), (w_in, w_ref))
        )
    ]
    for copy in brought:
        copy.start()

    for copy in brought[:2]:
        copy.wait()
    piece = jnp.zeros((SUB, LANE), F32)
    for c in range(4):
        row, tok = iota((SUB, TOK), 0), iota((SUB, TOK), 1)
        pick = jnp.where((row - c * BLK) == (tok >> 6), 1.0, 0.0).astype(BF16)
        src = k_ref if c < 2 else v_ref
        piece += dot_nn(pick, src[:, (c % 2) * LANE : (c % 2 + 1) * LANE])
    fine[w.xh * n * n] = (piece * 0.125).astype(BF16)
    pl.semaphore_wait(barrier, 4 * (n - 1) + 3 + tps - 1)

    def move_halo(copy):
        for src, pad in ((k_ref, kpad), (v_ref, vpad)):
            copy(src.at[pl.ds(half, half)], pad.at[pl.ds(0, half)], w.step(1))
            copy(src.at[pl.ds(0, half)], pad.at[pl.ds(half + TOK, half)], w.step(-1))

    def move_columns(copy):
        for k in range(1, tps):
            copy(og_ref, ogs.at[w.tp], w.tp_at(k)[1])

    summaries = Gather(log, w, fine)
    halo = Flight(log, move_halo, kpad)
    columns = Flight(log, move_columns, ogs.at[pl.ds(0, tps - 1)])
    summaries.begin()
    halo.begin()
    brought[2].wait()
    columns.begin()

    ogs[w.tp] = og_ref[...]
    kpad[half : half + TOK] = k_ref[...]
    vpad[half : half + TOK] = v_ref[...]
    gkpad[...] = jnp.zeros_like(gkpad)
    gvpad[...] = jnp.zeros_like(gvpad)
    dtop[...] = jnp.zeros_like(dtop)
    for copy in brought[3:]:
        copy.wait()

    bits = n.bit_length() - 1
    place = iota((1, tiles), 1)

    def ahead(slot):
        return jnp.where((slot & 1) == 1, (slot + 1) >> 1, n - (slot >> 1))

    by_row, by_col = ahead((place >> bits) & (n - 1)), ahead(place & (n - 1))
    tile_of = jnp.where(
        place < n * n,
        ((w.z + by_col) & (n - 1)) * (2 * n) + ((w.y + by_row) & (n - 1)) * 2,
        ((w.z + by_row) & (n - 1)) * (2 * n) + ((w.y + by_col) & (n - 1)) * 2 + 1,
    )
    rows8 = iota((8, tiles), 0)
    listed = []
    for g in range(BLK * C1 // 8):
        wanted = jnp.zeros((8, tiles), jnp.int32)
        for i in range(8):
            at = g * 8 + i
            wanted = jnp.where(rows8 == i, cpl_ref[at // C1, at % C1], wanted)
        listed.append(wanted)
    wanted = jnp.concatenate(listed, 0)
    hot[...] = jnp.where(wanted == tile_of, 1.0, 0.0).astype(BF16)

    size = group * SUB
    to, fro = iota((size, size), 0), iota((size, size), 1)
    gbits = group.bit_length() - 1
    swapped = (fro & (SUB - 1)) * group + (fro >> 4)
    swap = jnp.where(to == swapped, 1.0, 0.0).astype(BF16)
    swapped = (fro & (group - 1)) * SUB + (fro >> gbits)
    swap_back = jnp.where(to == swapped, 1.0, 0.0).astype(BF16)

    head_of = iota((1, COLS), 1) >> 6
    masks = [jnp.where(head_of == h, 1.0, 0.0) for h in range(HEADS)]
    masks_b = [m.astype(BF16) for m in masks]

    def diagonal(rows):
        return jnp.concatenate([rows * m for m in masks_b], 0)

    def collect(full):
        out = full[0:NB] * masks[0]
        for h in range(1, HEADS):
            out += full[h * NB : (h + 1) * NB] * masks[h]
        return out

    summaries.forward()

    spots = w.spots()
    halo.land()
    for b in range(BLK):
        scores = dot_nt(kpad[b * NB : b * NB + NEAR], diagonal(q_ref[b * NB : (b + 1) * NB])) * 0.125
        for d in range(5):
            target = w.seq * BLK + b + d - 2
            chosen = (off_ref[b, 0] == d - 2) | (off_ref[b, 1] == d - 2) | (off_ref[b, 2] == d - 2)
            usable = chosen & (target >= 0) & (target < nblk)
            probs[b, d * NB : (d + 1) * NB] = scores[d * NB : (d + 1) * NB] + jnp.where(usable, 0.0, -1e30)
    summaries.land()

    packed = jnp.concatenate([fine[g * group : (g + 1) * group].reshape(size, LANE) for g in range(groups)], 1)
    by_row = dot_nn(swap, packed)
    flat = jnp.concatenate(
        [
            jnp.concatenate([by_row[s * group : (s + 1) * group, g * LANE : (g + 1) * LANE] for s in range(SUB)], 1)
            for g in range(groups)
        ],
        0,
    )
    tops = []
    for c in range(4):
        total = flat[:, c * BLK * LANE : (c * BLK + 1) * LANE]
        for r in range(1, BLK):
            total += flat[:, (c * BLK + r) * LANE : (c * BLK + r + 1) * LANE]
        tops.append((total * 0.5).astype(BF16))
    far = dot_nn(hot[...], flat.astype(BF16)).astype(BF16)
    for b in range(BLK):
        for r in range(BLK):
            for c in range(4):
                s = c * BLK + r
                into = kft if c < 2 else vft
                into[b, r * C1 : (r + 1) * C1, (c % 2) * LANE : (c % 2 + 1) * LANE] = far[
                    b * C1 : (b + 1) * C1, s * LANE : (s + 1) * LANE
                ]
        kft[b, FAR:, :LANE], kft[b, FAR:, LANE:] = tops[0], tops[1]
        vft[b, FAR:, :LANE], vft[b, FAR:, LANE:] = tops[2], tops[3]

    def listed_rows(pad, rest, b):
        return jnp.concatenate([pad[b * NB : b * NB + NEAR], rest[b]], 0)

    for b in range(BLK):
        vals = listed_rows(vpad, vft, b)
        rest = dot_nt(kft[b], diagonal(q_ref[b * NB : (b + 1) * NB])) * 0.125
        scores = jnp.concatenate([probs[b, :NEAR], rest], 0)
        peak = jnp.max(scores, 0, keepdims=True)
        exps = jnp.exp(scores - peak)
        prob = exps * (1.0 / jnp.sum(exps, 0, keepdims=True))
        prob_b = prob.astype(BF16)
        probs[b] = prob
        halves[b] = prob_b
        att[b * NB : (b + 1) * NB] = collect(dot_tn(prob_b, vals)).astype(BF16)

    columns.land()
    for t in range(tps):
        part = dot_tn(att[...], ogs[t]).astype(BF16)
        for j in range(COLS // LANE):
            for i in range(TOK // SUB):
                wpart[spots[(t * 2 + j) * 16 + i]] = part[i * SUB : (i + 1) * SUB, j * LANE : (j + 1) * LANE]
    weight = Scatter(log, w, wpart, wgot1, wrows, wgot2, 5 if n == 8 else n - 1)
    whole = Gather(log, w, wfull)
    weight.begin()

    for t in range(tps):
        msend[t] = dot_nn(att[...], w_ref[:, t * COLS : (t + 1) * COLS]).astype(BF16)

    def move_mix(copy):
        for k in range(1, tps):
            c, device = w.tp_at(k)
            copy(msend.at[c], mgot.at[k], device)

    mix = Flight(log, move_mix, mgot.at[pl.ds(0, tps - 1)])
    mix.begin()
    mine_out[...] = dot_nn(att[...], w_ref[:, pl.ds(pl.multiple_of(w.tp * COLS, COLS), COLS)])

    grad = dot_nt(ogs[0], w_ref[:, 0:COLS])
    for t in range(1, tps):
        grad += dot_nt(ogs[t], w_ref[:, t * COLS : (t + 1) * COLS])
    gatt[...] = grad.astype(BF16)

    for b in range(BLK):
        keys = listed_rows(kpad, kft, b)
        vals = listed_rows(vpad, vft, b)
        q_diag = diagonal(q_ref[b * NB : (b + 1) * NB])
        g_diag = diagonal(gatt[b * NB : (b + 1) * NB])
        prob = probs[b]
        dprob = dot_nt(vals, g_diag)
        inner = jnp.sum(prob * dprob, 0, keepdims=True)
        dscore = (prob * (dprob - inner) * 0.125).astype(BF16)
        gq_ref[b * NB : (b + 1) * NB] = collect(dot_tn(dscore, keys)).astype(BF16)
        dkey = dot_nn(dscore, q_diag)
        dval = dot_nn(halves[b], g_diag)
        gkpad[b * NB : b * NB + NEAR] += dkey[:NEAR]
        gvpad[b * NB : b * NB + NEAR] += dval[:NEAR]
        for r in range(BLK):
            for c in range(4):
                s = c * BLK + r
                src = dkey if c < 2 else dval
                dlist[b * C1 : (b + 1) * C1, s * LANE : (s + 1) * LANE] = src[
                    NEAR + r * C1 : NEAR + (r + 1) * C1, (c % 2) * LANE : (c % 2 + 1) * LANE
                ].astype(BF16)
        dtop[:, :COLS] += dkey[NEAR + FAR :]
        dtop[:, COLS:] += dval[NEAR + FAR :]

    for i, pad in enumerate((gkpad, gvpad)):
        hsend[i] = pad[half + TOK :].astype(BF16)
        hsend[2 + i] = pad[:half].astype(BF16)

    def move_back(copy):
        for i in range(2):
            copy(hsend.at[i], hgot.at[i], w.step(1))
            copy(hsend.at[2 + i], hgot.at[2 + i], w.step(-1))

    tile_grad = dot_tn(hot[...], dlist[...])
    cols = []
    for c in range(4):
        for r in range(BLK):
            s = c * BLK + r
            cols.append(tile_grad[:, s * LANE : (s + 1) * LANE] + dtop[:, c * LANE : (c + 1) * LANE] * 0.5)
    by_row = jnp.concatenate(
        [
            jnp.concatenate([cols[s][g * group : (g + 1) * group] for s in range(SUB)], 0)
            for g in range(groups)
        ],
        1,
    ).astype(BF16)
    packed = dot_nn(swap_back, by_row).astype(BF16)
    for g in range(groups):
        fpart[g * group : (g + 1) * group] = packed[:, g * LANE : (g + 1) * LANE].reshape(group, SUB, LANE)
    halo_back = Flight(log, move_back, hgot)
    halo_back.begin()
    coupled = Scatter(log, w, fpart, fgot1, frows, fgot2, 0)

    weight.forward()
    coupled.begin()

    mix.land()
    total = mine_out[...]
    for k in range(1, tps):
        total += mgot[k].astype(F32)
    mixed_ref[...] = total.astype(BF16)
    halo_back.land()

    wfull[w.xh * n * n] = weight.land().astype(BF16)
    whole.begin()
    coupled.forward()
    whole.forward()

    fine_grad = coupled.land() * 0.125
    for i, (pad, out) in enumerate(((gkpad, gk_ref), (gvpad, gv_ref))):
        for r in range(BLK):
            rows = pad[half + r * NB : half + (r + 1) * NB]
            if r < BLK // 2:
                rows += hgot[i, r * NB : (r + 1) * NB].astype(F32)
            else:
                rows += hgot[2 + i, r * NB - half : (r + 1) * NB - half].astype(F32)
            for c in range(2):
                s = (2 * i + c) * BLK + r
                out[r * NB : (r + 1) * NB, c * LANE : (c + 1) * LANE] = (
                    rows[:, c * LANE : (c + 1) * LANE] + fine_grad[s : s + 1]
                ).astype(BF16)

    for flight in log.flights:
        if flight not in whole.onward:
            flight.end()
    whole.land()
    pieces_ref[...] = wfull[...]
    for onward in whole.onward:
        onward.end()


def hand_over(n, tps, *refs):
    held, pieces, made, weight, sems = refs[:4], refs[4], refs[5:10], *refs[10:]
    out = [pltpu.make_async_copy(src, dst, sems.at[i]) for i, (src, dst) in enumerate(zip(held, made))]
    for copy in out:
        copy.start()
    spots = Place(n, tps).spots()
    for j in range(tps * COLS // LANE):
        cols = pl.ds(j * LANE, LANE)
        for i in range(TOK // SUB):
            weight[i * SUB : (i + 1) * SUB, cols] = pieces[spots[j * 16 + i]].astype(F32)
        out.append(pltpu.make_async_copy(weight.at[:, cols], made[4].at[:, cols], sems.at[4 + j]))
        out[-1].start()
    for copy in out:
        copy.wait()


def shards(n, tps, queries, keys, values, out_weight, out_grad, near_offsets, coupling):
    tiles = 2 * n * n
    group = min(16, tiles)
    pieces = (tiles, SUB, LANE)
    dma = lambda *shape: pltpu.SemaphoreType.DMA(shape)
    vm = lambda dtype, *shape: pltpu.VMEM(shape, dtype)
    in_vmem = pl.BlockSpec(memory_space=pltpu.VMEM)
    in_place = pl.BlockSpec(memory_space=pltpu.HBM)
    rest = FAR + tiles
    length = NEAR + rest
    sums = [vm(BF16, *pieces), vm(BF16, 2, n, n, SUB, LANE), vm(BF16, 2, n, SUB, LANE), vm(BF16, 2, n, SUB, LANE)]
    scratch = [
        pltpu.SMEM(near_offsets.shape, jnp.int32), pltpu.SMEM(coupling.shape, jnp.int32),
        *(vm(BF16, *x.shape) for x in (queries, keys, values, out_weight, out_grad)), dma(7),
        vm(BF16, 2 * TOK, COLS), vm(BF16, 2 * TOK, COLS), vm(BF16, *pieces), vm(BF16, tps, TOK, COLS),
        vm(BF16, BLK, rest, COLS), vm(BF16, BLK, rest, COLS), vm(BF16, BLK * C1, tiles),
        vm(F32, BLK, length, COLS), vm(BF16, BLK, length, COLS), vm(BF16, TOK, COLS), vm(BF16, TOK, COLS), vm(F32, TOK, COLS),
        vm(BF16, tps, TOK, COLS), vm(BF16, tps, TOK, COLS), vm(F32, 2 * TOK, COLS), vm(F32, 2 * TOK, COLS),
        vm(BF16, 4, TOK // 2, COLS), vm(BF16, 4, TOK // 2, COLS), vm(BF16, BLK * C1, SUB * LANE), vm(F32, tiles, 2 * COLS),
        *sums, vm(BF16, *pieces), *sums,
        dma(SENDS), dma(RECVS),
    ]
    like = lambda x: jax.ShapeDtypeStruct(x.shape, BF16)
    shapes = (like(out_grad), like(queries), like(keys), like(values))
    weight_grad = jax.ShapeDtypeStruct(out_weight.shape, F32)
    results = pl.pallas_call(
        functools.partial(kernel, n, tps, group),
        out_shape=(*(pltpu.VMEM(x.shape, BF16) for x in shapes), pltpu.VMEM(pieces, BF16)),
        in_specs=[in_place] * 7,
        out_specs=[in_vmem] * 5,
        scratch_shapes=scratch,
        compiler_params=pltpu.CompilerParams(collective_id=0, has_side_effects=True, vmem_limit_bytes=VMEM),
    )(*(
        pltpu.with_memory_space_constraint(x, pltpu.HBM)
        for x in (near_offsets, coupling, queries, keys, values, out_weight, out_grad)
    ))
    return pl.pallas_call(
        functools.partial(hand_over, n, tps),
        out_shape=(*shapes, weight_grad),
        in_specs=[in_vmem] * 5,
        out_specs=[in_place] * 5,
        scratch_shapes=[vm(F32, *out_weight.shape), dma(4 + tps * COLS // LANE)],
        compiler_params=pltpu.CompilerParams(vmem_limit_bytes=VMEM),
    )(*results)


def solution(mesh):
    n = int(round((mesh.shape["seq"] // 2) ** 0.5))
    step = functools.partial(shards, n, mesh.shape["tp"])
    in_specs = (
        P("seq", "tp"),
        P("seq", "tp"),
        P("seq", "tp"),
        P("tp", None),
        P("seq", "tp"),
        P("seq", None),
        P("seq", None),
    )
    out_specs = (P("seq", "tp"), P("seq", "tp"), P("seq", "tp"), P("seq", "tp"), P("tp", None))
    return jax.shard_map(step, mesh=mesh, in_specs=in_specs, out_specs=out_specs, check_vma=False)
```

```python
import functools

import jax
import jax.numpy as jnp
from jax import lax
from jax.experimental import pallas as pl
from jax.experimental.pallas import tpu as pltpu
from jax.sharding import PartitionSpec as P

MESH = pl.DeviceIdType.MESH
F32 = jnp.float32
BF16 = jnp.bfloat16
HD = 64
NB = 64
BLK = 4
HEADS = 4
COLS = HEADS * HD
TOK = BLK * NB
C1 = 16
LANE = 128
SUB = 16
NEAR = 5 * NB
FAR = C1 * BLK
VMEM = 48 * 1024 * 1024
SENDS, RECVS = 22, 26


def each(low, high, body):
    for k in range(high - 1, low - 1, -1):
        body(k)


def dot_nn(a, b):
    return lax.dot_general(a, b, (((1,), (0,)), ((), ())), preferred_element_type=F32)


def dot_nt(a, b):
    return lax.dot_general(a, b, (((1,), (1,)), ((), ())), preferred_element_type=F32)


def dot_tn(a, b):
    return lax.dot_general(a, b, (((0,), (0,)), ((), ())), preferred_element_type=F32)


def iota(shape, dim):
    return lax.broadcasted_iota(jnp.int32, shape, dim)


class Place:
    def __init__(self, n, tps):
        self.n, self.tps = n, tps
        self.seqs = 2 * n * n
        self.seq = lax.axis_index("seq")
        self.tp = lax.axis_index("tp")
        self.z = lax.div(self.seq, 2 * n)
        self.y = lax.rem(lax.div(self.seq, 2), n)
        self.xh = lax.rem(self.seq, 2)
        self.mine = self.z * (1 - self.xh) + self.y * self.xh
        self.cross = self.y * (1 - self.xh) + self.z * self.xh

    def by(self, slot):
        return (slot + 1) // 2 if slot % 2 else self.n - slot // 2

    def back(self, slot):
        return slot if slot == self.n - 1 else slot + 1 if slot % 2 else slot - 1

    def slot(self, ahead):
        n = self.n
        upper = lax.div(n - 1 + n // 2 - ahead, n - 1)
        return upper * (2 * ahead - 1) + (1 - upper) * 2 * (n - ahead) + lax.div(n - 1 - ahead, n - 1)

    def at(self, z, y, xh):
        return (z * (2 * self.n) + y * 2 + xh, self.tp)

    def along_mine(self, slot, xh):
        c = lax.rem(self.mine + self.by(slot), self.n)
        return self.at(c * (1 - self.xh) + self.z * self.xh, self.y * (1 - self.xh) + c * self.xh, xh)

    def along_cross(self, slot, xh):
        c = lax.rem(self.cross + self.by(slot), self.n)
        return self.at(self.z * (1 - self.xh) + c * self.xh, c * (1 - self.xh) + self.y * self.xh, xh)

    def along_y(self, slot):
        return self.at(self.z, lax.rem(self.y + self.by(slot), self.n), self.xh)

    def along_z(self, slot):
        return self.at(lax.rem(self.z + self.by(slot), self.n), self.y, self.xh)

    def step(self, by):
        return (lax.rem(self.seq + self.seqs + by, self.seqs), self.tp)

    def tp_at(self, k):
        c = lax.rem(self.tp + k, self.tps)
        return c, (self.seq, c)

    def spots(self):
        n = self.n
        of_y = [self.slot(lax.rem(c + n - self.y, n)) for c in range(n)]
        of_z = [self.slot(lax.rem(c + n - self.z, n)) for c in range(n)]
        return [
            h * n * n + (of_z if h else of_y)[r] * n + (of_y if h else of_z)[c]
            for h in range(2)
            for r in range(n)
            for c in range(n)
        ]


def remote(src, dst, send, recv, device):
    return pltpu.make_async_remote_copy(
        src_ref=src, dst_ref=dst, send_sem=send, recv_sem=recv, device_id=device, device_id_type=MESH
    )


class Log:
    def __init__(self, w, sends, recvs):
        self.w, self.sends, self.recvs = w, sends, recvs
        self.flights, self.sent, self.received = [], 0, 0

    def send(self):
        self.sent += 1
        return self.sends.at[self.sent - 1]

    def recv(self):
        self.received += 1
        return self.recvs.at[self.received - 1]

    def wait(self, size, send, recv):
        return remote(size, size, send, recv, self.w.at(self.w.z, self.w.y, 1 - self.w.xh))


class Flight:
    def __init__(self, log, move, size, recv=None):
        self.log, self.move, self.size = log, move, size
        self.send, self.recv = log.send(), log.recv() if recv is None else recv
        log.flights.append(self)

    def begin(self):
        self.move(lambda src, dst, device: remote(src, dst, self.send, self.recv, device).start())

    def land(self):
        self.log.wait(self.size, self.send, self.recv).wait_recv()

    def end(self):
        self.log.wait(self.size, self.send, self.recv).wait_send()


class Spread:
    def __init__(self, log, w, buf, other, steps):
        self.log, self.w, self.buf, self.other = log, w, buf, other
        self.send = log.send()
        self.recvs = {step: log.recv() for step in steps}
        log.flights.append(self)

    def count(self, low, high):
        return high - max(low, 1) + (1 if self.other and low == 0 else 0)

    def begin(self):
        w = self.w
        own = self.buf.at[w.xh * w.n * w.n]
        xh = 1 - w.xh if self.other else w.xh
        for i in range(w.n - 1, -1 if self.other else 0, -1):
            j = w.back(i) if i else 0
            recv = next(sem for (low, high), sem in self.recvs.items() if low <= j < high)
            into = self.buf.at[w.xh * w.n * w.n + j]
            device = w.along_mine(i, xh) if i else w.at(w.z, w.y, xh)
            remote(own, into, self.send, recv, device).start()

    def land(self, low, high):
        size = self.buf.at[pl.ds(0, self.count(low, high))]
        self.log.wait(size, self.send, self.recvs[low, high]).wait_recv()

    def end(self):
        size = self.buf.at[pl.ds(0, self.count(0, self.w.n))]
        self.log.wait(size, self.send, next(iter(self.recvs.values()))).wait_send()


class Gather:
    def __init__(self, log, w, buf):
        n = w.n
        self.w, self.buf = w, buf
        cuts = [c for c in (1, 5, 8) if c < n] + [n]
        same = list(zip([0] + cuts[:-1], cuts))
        cross = [(0, cuts[1])] + same[2:]
        self.out = [Spread(log, w, buf, 0, same[1:]), Spread(log, w, buf, 1, cross)]
        self.steps = [(0, *part) for part in same] + [(1, *part) for part in cross]
        self.steps.sort(key=lambda step: (step[1] + 2 * step[0], step[0]))
        self.onward = [self.relay(log, *step) for step in self.steps]

    def relay(self, log, other, low, high):
        w, n, buf = self.w, self.w.n, self.buf
        base = (1 - w.xh if other else w.xh) * n * n
        mine = buf.at[pl.ds(base + low, high - low)]

        def move(copy):
            for i in range(n - 1, 0, -1):
                into = buf.at[pl.ds(base + w.back(i) * n + low, high - low)]
                copy(mine, into, (w.along_mine if other else w.along_cross)(i, w.xh))

        return Flight(log, move, buf.at[pl.ds(0, (n - 1) * (high - low))])

    def begin(self):
        self.out[1].begin()
        self.out[0].begin()
        self.onward[0].begin()

    def forward(self):
        for (other, low, high), onward in zip(self.steps[1:], self.onward[1:]):
            self.out[other].land(low, high)
            onward.begin()

    def land(self):
        for onward in self.onward:
            onward.land()


class Scatter:
    def __init__(self, log, w, part, got_1, rows, got_2, cut):
        n = w.n
        self.w, self.part, self.got_1, self.rows, self.got_2 = w, part, got_1, rows, got_2
        self.cols = [(cut, n), (0, cut)] if cut else [(0, n)]
        self.first = [self.to_rows(log, *c) for c in self.cols]
        self.second = [self.to_owners(log, *c) for c in self.cols]

    def to_rows(self, log, low, high):
        w, n = self.w, self.w.n

        def move(copy):
            for i in range(n - 1, 0, -1):
                for h, device in ((0, w.along_y(i)), (1, w.along_z(i))):
                    mine = self.part.at[pl.ds(h * n * n + i * n + low, high - low)]
                    copy(mine, self.got_1.at[h, i, pl.ds(low, high - low)], device)

        return Flight(log, move, self.part.at[pl.ds(0, 2 * (n - 1) * (high - low))])

    def to_owners(self, log, low, high):
        w = self.w

        def move(copy):
            for i in range(high - 1, max(low, 1) - 1, -1):
                copy(self.rows.at[1 - w.xh, i], self.got_2.at[1, i], w.along_cross(i, 1 - w.xh))
            if low == 0:
                copy(self.rows.at[1 - w.xh, 0], self.got_2.at[1, 0], w.at(w.z, w.y, 1 - w.xh))
            for i in range(high - 1, max(low, 1) - 1, -1):
                copy(self.rows.at[w.xh, i], self.got_2.at[0, i], w.along_mine(i, w.xh))

        count = 2 * (high - max(low, 1)) + (1 if low == 0 else 0)
        return Flight(log, move, self.part.at[pl.ds(0, count)])

    def begin(self):
        for first in self.first:
            first.begin()

    def forward(self):
        n = self.w.n
        for (low, high), first, second in zip(self.cols, self.first, self.second):
            first.land()
            for h in range(2):
                total = self.part[h * n * n + low : h * n * n + high].astype(F32)
                for i in range(1, n):
                    total += self.got_1[h, i, low:high].astype(F32)
                self.rows[h, low:high] = total.astype(BF16)
            second.begin()

    def land(self):
        for second in self.second:
            second.land()
        total = self.rows[self.w.xh, 0].astype(F32)
        for i in range(1, self.w.n):
            total += self.got_2[0, i].astype(F32)
        for i in range(self.w.n):
            total += self.got_2[1, i].astype(F32)
        return total


def kernel(
    n, tps, group,
    off_in, cpl_in, q_in, k_in, v_in, w_in, og_in,
    mixed_ref, gq_ref, gk_ref, gv_ref, pieces_ref,
    off_ref, cpl_ref, q_ref, k_ref, v_ref, w_ref, og_ref, s_in,
    kpad, vpad, fine, ogs, kft, vft, hot, probs, halves, att, gatt, mine_out,
    msend, mgot, gkpad, gvpad, hsend, hgot, dlist, dtop,
    wpart, wgot1, wrows, wgot2, wfull, fpart, fgot1, frows, fgot2,
    sends, recvs,
):
    w = Place(n, tps)
    tiles = w.seqs
    groups = tiles // group
    nblk = tiles * BLK
    half = TOK // 2
    log = Log(w, sends, recvs)

    barrier = pltpu.get_barrier_semaphore()

    def greet(device):
        pl.semaphore_signal(barrier, inc=1, device_id=device, device_id_type=MESH)

    def greet_square(i):
        greet(w.along_y(i))
        greet(w.along_z(i))
        greet(w.along_mine(i, 1 - w.xh))
        greet(w.along_cross(i, 1 - w.xh))

    each(1, n, greet_square)
    greet(w.at(w.z, w.y, 1 - w.xh))
    greet(w.step(1))
    greet(w.step(-1))
    each(1, tps, lambda k: greet(w.tp_at(k)[1]))

    brought = [
        pltpu.make_async_copy(src, dst, s_in.at[i])
        for i, (src, dst) in enumerate(
            ((k_in, k_ref), (v_in, v_ref), (og_in, og_ref), (cpl_in, cpl_ref), (off_in, off_ref), (q_in, q_ref), (w_in, w_ref))
        )
    ]
    for copy in brought:
        copy.start()

    for copy in brought[:2]:
        copy.wait()
    piece = jnp.zeros((SUB, LANE), F32)
    for c in range(4):
        row, tok = iota((SUB, TOK), 0), iota((SUB, TOK), 1)
        pick = jnp.where((row - c * BLK) == (tok >> 6), 1.0, 0.0).astype(BF16)
        src = k_ref if c < 2 else v_ref
        piece += dot_nn(pick, src[:, (c % 2) * LANE : (c % 2 + 1) * LANE])
    fine[w.xh * n * n] = (piece * 0.125).astype(BF16)
    pl.semaphore_wait(barrier, 4 * (n - 1) + 3 + tps - 1)

    def move_halo(copy):
        for src, pad in ((k_ref, kpad), (v_ref, vpad)):
            copy(src.at[pl.ds(half, half)], pad.at[pl.ds(0, half)], w.step(1))
            copy(src.at[pl.ds(0, half)], pad.at[pl.ds(half + TOK, half)], w.step(-1))

    def move_columns(copy):
        for k in range(1, tps):
            copy(og_ref, ogs.at[w.tp], w.tp_at(k)[1])

    summaries = Gather(log, w, fine)
    halo = Flight(log, move_halo, kpad)
    columns = Flight(log, move_columns, ogs.at[pl.ds(0, tps - 1)])
    summaries.begin()
    halo.begin()
    brought[2].wait()
    columns.begin()

    ogs[w.tp] = og_ref[...]
    kpad[half : half + TOK] = k_ref[...]
    vpad[half : half + TOK] = v_ref[...]
    gkpad[...] = jnp.zeros_like(gkpad)
    gvpad[...] = jnp.zeros_like(gvpad)
    dtop[...] = jnp.zeros_like(dtop)
    for copy in brought[3:]:
        copy.wait()

    bits = n.bit_length() - 1
    place = iota((1, tiles), 1)

    def ahead(slot):
        return jnp.where((slot & 1) == 1, (slot + 1) >> 1, n - (slot >> 1))

    by_row, by_col = ahead((place >> bits) & (n - 1)), ahead(place & (n - 1))
    tile_of = jnp.where(
        place < n * n,
        ((w.z + by_col) & (n - 1)) * (2 * n) + ((w.y + by_row) & (n - 1)) * 2,
        ((w.z + by_row) & (n - 1)) * (2 * n) + ((w.y + by_col) & (n - 1)) * 2 + 1,
    )
    rows8 = iota((8, tiles), 0)
    listed = []
    for g in range(BLK * C1 // 8):
        wanted = jnp.zeros((8, tiles), jnp.int32)
        for i in range(8):
            at = g * 8 + i
            wanted = jnp.where(rows8 == i, cpl_ref[at // C1, at % C1], wanted)
        listed.append(wanted)
    wanted = jnp.concatenate(listed, 0)
    hot[...] = jnp.where(wanted == tile_of, 1.0, 0.0).astype(BF16)

    size = group * SUB
    to, fro = iota((size, size), 0), iota((size, size), 1)
    gbits = group.bit_length() - 1
    swapped = (fro & (SUB - 1)) * group + (fro >> 4)
    swap = jnp.where(to == swapped, 1.0, 0.0).astype(BF16)
    swapped = (fro & (group - 1)) * SUB + (fro >> gbits)
    swap_back = jnp.where(to == swapped, 1.0, 0.0).astype(BF16)

    head_of = iota((1, COLS), 1) >> 6
    masks = [jnp.where(head_of == h, 1.0, 0.0) for h in range(HEADS)]
    masks_b = [m.astype(BF16) for m in masks]

    def diagonal(rows):
        return jnp.concatenate([rows * m for m in masks_b], 0)

    def collect(full):
        out = full[0:NB] * masks[0]
        for h in range(1, HEADS):
            out += full[h * NB : (h + 1) * NB] * masks[h]
        return out

    summaries.forward()

    spots = w.spots()
    halo.land()
    for b in range(BLK):
        scores = dot_nt(kpad[b * NB : b * NB + NEAR], diagonal(q_ref[b * NB : (b + 1) * NB])) * 0.125
        for d in range(5):
            target = w.seq * BLK + b + d - 2
            chosen = (off_ref[b, 0] == d - 2) | (off_ref[b, 1] == d - 2) | (off_ref[b, 2] == d - 2)
            usable = chosen & (target >= 0) & (target < nblk)
            probs[b, d * NB : (d + 1) * NB] = scores[d * NB : (d + 1) * NB] + jnp.where(usable, 0.0, -1e30)
    summaries.land()

    packed = jnp.concatenate([fine[g * group : (g + 1) * group].reshape(size, LANE) for g in range(groups)], 1)
    by_row = dot_nn(swap, packed)
    flat = jnp.concatenate(
        [
            jnp.concatenate([by_row[s * group : (s + 1) * group, g * LANE : (g + 1) * LANE] for s in range(SUB)], 1)
            for g in range(groups)
        ],
        0,
    )
    tops = []
    for c in range(4):
        total = flat[:, c * BLK * LANE : (c * BLK + 1) * LANE]
        for r in range(1, BLK):
            total += flat[:, (c * BLK + r) * LANE : (c * BLK + r + 1) * LANE]
        tops.append((total * 0.5).astype(BF16))
    far = dot_nn(hot[...], flat.astype(BF16)).astype(BF16)
    for b in range(BLK):
        for r in range(BLK):
            for c in range(4):
                s = c * BLK + r
                into = kft if c < 2 else vft
                into[b, r * C1 : (r + 1) * C1, (c % 2) * LANE : (c % 2 + 1) * LANE] = far[
                    b * C1 : (b + 1) * C1, s * LANE : (s + 1) * LANE
                ]
        kft[b, FAR:, :LANE], kft[b, FAR:, LANE:] = tops[0], tops[1]
        vft[b, FAR:, :LANE], vft[b, FAR:, LANE:] = tops[2], tops[3]

    def listed_rows(pad, rest, b):
        return jnp.concatenate([pad[b * NB : b * NB + NEAR], rest[b]], 0)

    for b in range(BLK):
        vals = listed_rows(vpad, vft, b)
        rest = dot_nt(kft[b], diagonal(q_ref[b * NB : (b + 1) * NB])) * 0.125
        scores = jnp.concatenate([probs[b, :NEAR], rest], 0)
        peak = jnp.max(scores, 0, keepdims=True)
        exps = jnp.exp(scores - peak)
        prob = exps * (1.0 / jnp.sum(exps, 0, keepdims=True))
        prob_b = prob.astype(BF16)
        probs[b] = prob
        halves[b] = prob_b
        att[b * NB : (b + 1) * NB] = collect(dot_tn(prob_b, vals)).astype(BF16)

    columns.land()
    for t in range(tps):
        part = dot_tn(att[...], ogs[t]).astype(BF16)
        for j in range(COLS // LANE):
            for i in range(TOK // SUB):
                wpart[spots[(t * 2 + j) * 16 + i]] = part[i * SUB : (i + 1) * SUB, j * LANE : (j + 1) * LANE]
    weight = Scatter(log, w, wpart, wgot1, wrows, wgot2, 0)
    whole = Gather(log, w, wfull)
    weight.begin()

    for t in range(tps):
        msend[t] = dot_nn(att[...], w_ref[:, t * COLS : (t + 1) * COLS]).astype(BF16)

    def move_mix(copy):
        for k in range(1, tps):
            c, device = w.tp_at(k)
            copy(msend.at[c], mgot.at[k], device)

    mix = Flight(log, move_mix, mgot.at[pl.ds(0, tps - 1)])
    mix.begin()
    mine_out[...] = dot_nn(att[...], w_ref[:, pl.ds(pl.multiple_of(w.tp * COLS, COLS), COLS)])

    grad = dot_nt(ogs[0], w_ref[:, 0:COLS])
    for t in range(1, tps):
        grad += dot_nt(ogs[t], w_ref[:, t * COLS : (t + 1) * COLS])
    gatt[...] = grad.astype(BF16)

    for b in range(BLK):
        keys = listed_rows(kpad, kft, b)
        vals = listed_rows(vpad, vft, b)
        q_diag = diagonal(q_ref[b * NB : (b + 1) * NB])
        g_diag = diagonal(gatt[b * NB : (b + 1) * NB])
        prob = probs[b]
        dprob = dot_nt(vals, g_diag)
        inner = jnp.sum(prob * dprob, 0, keepdims=True)
        dscore = (prob * (dprob - inner) * 0.125).astype(BF16)
        gq_ref[b * NB : (b + 1) * NB] = collect(dot_tn(dscore, keys)).astype(BF16)
        dkey = dot_nn(dscore, q_diag)
        dval = dot_nn(halves[b], g_diag)
        gkpad[b * NB : b * NB + NEAR] += dkey[:NEAR]
        gvpad[b * NB : b * NB + NEAR] += dval[:NEAR]
        for r in range(BLK):
            for c in range(4):
                s = c * BLK + r
                src = dkey if c < 2 else dval
                dlist[b * C1 : (b + 1) * C1, s * LANE : (s + 1) * LANE] = src[
                    NEAR + r * C1 : NEAR + (r + 1) * C1, (c % 2) * LANE : (c % 2 + 1) * LANE
                ].astype(BF16)
        dtop[:, :COLS] += dkey[NEAR + FAR :]
        dtop[:, COLS:] += dval[NEAR + FAR :]

    for i, pad in enumerate((gkpad, gvpad)):
        hsend[i] = pad[half + TOK :].astype(BF16)
        hsend[2 + i] = pad[:half].astype(BF16)

    def move_back(copy):
        for i in range(2):
            copy(hsend.at[i], hgot.at[i], w.step(1))
            copy(hsend.at[2 + i], hgot.at[2 + i], w.step(-1))

    tile_grad = dot_tn(hot[...], dlist[...])
    cols = []
    for c in range(4):
        for r in range(BLK):
            s = c * BLK + r
            cols.append(tile_grad[:, s * LANE : (s + 1) * LANE] + dtop[:, c * LANE : (c + 1) * LANE] * 0.5)
    by_row = jnp.concatenate(
        [
            jnp.concatenate([cols[s][g * group : (g + 1) * group] for s in range(SUB)], 0)
            for g in range(groups)
        ],
        1,
    ).astype(BF16)
    packed = dot_nn(swap_back, by_row).astype(BF16)
    for g in range(groups):
        fpart[g * group : (g + 1) * group] = packed[:, g * LANE : (g + 1) * LANE].reshape(group, SUB, LANE)
    halo_back = Flight(log, move_back, hgot)
    halo_back.begin()
    coupled = Scatter(log, w, fpart, fgot1, frows, fgot2, 0)

    weight.forward()
    coupled.begin()

    wfull[w.xh * n * n] = weight.land().astype(BF16)
    whole.begin()
    coupled.forward()
    whole.forward()

    mix.land()
    total = mine_out[...]
    for k in range(1, tps):
        total += mgot[k].astype(F32)
    mixed_ref[...] = total.astype(BF16)
    halo_back.land()

    fine_grad = coupled.land() * 0.125
    for i, (pad, out) in enumerate(((gkpad, gk_ref), (gvpad, gv_ref))):
        for r in range(BLK):
            rows = pad[half + r * NB : half + (r + 1) * NB]
            if r < BLK // 2:
                rows += hgot[i, r * NB : (r + 1) * NB].astype(F32)
            else:
                rows += hgot[2 + i, r * NB - half : (r + 1) * NB - half].astype(F32)
            for c in range(2):
                s = (2 * i + c) * BLK + r
                out[r * NB : (r + 1) * NB, c * LANE : (c + 1) * LANE] = (
                    rows[:, c * LANE : (c + 1) * LANE] + fine_grad[s : s + 1]
                ).astype(BF16)

    for flight in log.flights:
        if flight not in whole.onward:
            flight.end()
    whole.land()
    pieces_ref[...] = wfull[...]
    for onward in whole.onward:
        onward.end()


def hand_over(n, tps, *refs):
    held, pieces, made, weight, sems = refs[:4], refs[4], refs[5:10], *refs[10:]
    out = [pltpu.make_async_copy(src, dst, sems.at[i]) for i, (src, dst) in enumerate(zip(held, made))]
    for copy in out:
        copy.start()
    spots = Place(n, tps).spots()
    for j in range(tps * COLS // LANE):
        cols = pl.ds(j * LANE, LANE)
        for i in range(TOK // SUB):
            weight[i * SUB : (i + 1) * SUB, cols] = pieces[spots[j * 16 + i]].astype(F32)
        out.append(pltpu.make_async_copy(weight.at[:, cols], made[4].at[:, cols], sems.at[4 + j]))
        out[-1].start()
    for copy in out:
        copy.wait()


def shards(n, tps, queries, keys, values, out_weight, out_grad, near_offsets, coupling):
    tiles = 2 * n * n
    group = min(16, tiles)
    pieces = (tiles, SUB, LANE)
    dma = lambda *shape: pltpu.SemaphoreType.DMA(shape)
    vm = lambda dtype, *shape: pltpu.VMEM(shape, dtype)
    in_vmem = pl.BlockSpec(memory_space=pltpu.VMEM)
    in_place = pl.BlockSpec(memory_space=pltpu.HBM)
    rest = FAR + tiles
    length = NEAR + rest
    sums = [vm(BF16, *pieces), vm(BF16, 2, n, n, SUB, LANE), vm(BF16, 2, n, SUB, LANE), vm(BF16, 2, n, SUB, LANE)]
    scratch = [
        pltpu.SMEM(near_offsets.shape, jnp.int32), pltpu.SMEM(coupling.shape, jnp.int32),
        *(vm(BF16, *x.shape) for x in (queries, keys, values, out_weight, out_grad)), dma(7),
        vm(BF16, 2 * TOK, COLS), vm(BF16, 2 * TOK, COLS), vm(BF16, *pieces), vm(BF16, tps, TOK, COLS),
        vm(BF16, BLK, rest, COLS), vm(BF16, BLK, rest, COLS), vm(BF16, BLK * C1, tiles),
        vm(F32, BLK, length, COLS), vm(BF16, BLK, length, COLS), vm(BF16, TOK, COLS), vm(BF16, TOK, COLS), vm(F32, TOK, COLS),
        vm(BF16, tps, TOK, COLS), vm(BF16, tps, TOK, COLS), vm(F32, 2 * TOK, COLS), vm(F32, 2 * TOK, COLS),
        vm(BF16, 4, TOK // 2, COLS), vm(BF16, 4, TOK // 2, COLS), vm(BF16, BLK * C1, SUB * LANE), vm(F32, tiles, 2 * COLS),
        *sums, vm(BF16, *pieces), *sums,
        dma(SENDS), dma(RECVS),
    ]
    like = lambda x: jax.ShapeDtypeStruct(x.shape, BF16)
    shapes = (like(out_grad), like(queries), like(keys), like(values))
    weight_grad = jax.ShapeDtypeStruct(out_weight.shape, F32)
    results = pl.pallas_call(
        functools.partial(kernel, n, tps, group),
        out_shape=(*(pltpu.VMEM(x.shape, BF16) for x in shapes), pltpu.VMEM(pieces, BF16)),
        in_specs=[in_place] * 7,
        out_specs=[in_vmem] * 5,
        scratch_shapes=scratch,
        compiler_params=pltpu.CompilerParams(collective_id=0, has_side_effects=True, vmem_limit_bytes=VMEM),
    )(*(
        pltpu.with_memory_space_constraint(x, pltpu.HBM)
        for x in (near_offsets, coupling, queries, keys, values, out_weight, out_grad)
    ))
    return pl.pallas_call(
        functools.partial(hand_over, n, tps),
        out_shape=(*shapes, weight_grad),
        in_specs=[in_vmem] * 5,
        out_specs=[in_place] * 5,
        scratch_shapes=[vm(F32, *out_weight.shape), dma(4 + tps * COLS // LANE)],
        compiler_params=pltpu.CompilerParams(vmem_limit_bytes=VMEM),
    )(*results)


def solution(mesh):
    n = int(round((mesh.shape["seq"] // 2) ** 0.5))
    step = functools.partial(shards, n, mesh.shape["tp"])
    in_specs = (
        P("seq", "tp"),
        P("seq", "tp"),
        P("seq", "tp"),
        P("tp", None),
        P("seq", "tp"),
        P("seq", None),
        P("seq", None),
    )
    out_specs = (P("seq", "tp"), P("seq", "tp"), P("seq", "tp"), P("seq", "tp"), P("tp", None))
    return jax.shard_map(step, mesh=mesh, in_specs=in_specs, out_specs=out_specs, check_vma=False)
```
